512 devices in a mesh: dom: 128 (over z, y, core), rep: 4 (over x).
Axes of the slice: x: 4, y: 8, z: 8, core: 2. Of those that a mesh axis runs over, the one named last changes fastest.
Arguments:
- features: bfloat16 [262144, 768], P(('dom', 'rep')), may hold values from -13 to 13
- sketch_matrix: bfloat16 [768, 256], replicated, may hold values from -0.21875 to 0.21875
- tiles: bfloat16 [128, 20, 256, 256], P('dom'), may hold values from 0 to 2, as said below
- tile_dst: int32 [128, 20], P('dom'), may hold values from -1 to 7, as said below
- tile_src: int32 [128, 20], P('dom'), may hold values from 0 to 11, as said below
- halo_index: int32 [128, 1024], P('dom'), may hold values from 0 to 2047
- send_order: int32 [128, 2048], P('dom'), may hold values from 0 to 2047, each once within a row
- arrival_place: int32 [128, 2048], P('dom'), may hold values from 0 to 2047, each once within a row
Outputs:
- signals: bfloat16 [3, 256, 262144], P(None, 'rep', 'dom')
The draws below stay inside these ranges and needn't reach their ends.
Inputs may be any that keep to these rules, and one draw needn't show every extreme that they name: `tiles`: entries are zero or positive; in slot t < 8 of every partition the tile's diagonal is positive. `tile_dst`: in every partition slot t < 8 holds t, the live slots come first and the others hold -1; some partition uses every slot and some only the first 12. `tile_src`: slot t < 12 holds t in every partition; empty slots hold 0. `halo_index`: A row may be listed for several peers and more than once. `send_order`: each row is a permutation. `arrival_place`: each row is a permutation.
All inputs are finite; a program needn't handle non-finite values.
Results may differ from the reference program's by a relative error of at most 0.0034.
Values may be sent and summed in bfloat16 or wider, within the bound.
A program may use at most 64 MiB of HBM per device.

```python
import jax
import jax.numpy as jnp
from jax import lax

IN_WIDTH = 768
SKETCH = 256
TILE_SIDE = 256
ROWS_DEV = 2048
TILES_DEV = 20
HALO_ROWS = 1024
HALO_SLOT = 8
LAYOUT_SLOT = 16
NODE_COUNT = 262144
N_DOM = 128


def tile_lists(key):
    block_count = ROWS_DEV // TILE_SIDE
    halo_blocks = HALO_ROWS // TILE_SIDE
    spare = TILES_DEV - block_count - halo_blocks
    base = jax.random.fold_in(key, 7)
    first_key, second_key, third_key, fourth_key = jax.random.split(base, 4)
    spread = jax.random.randint(first_key, (N_DOM,), 0, spare + 1)
    extra = spread * spread // spare
    full_part = jax.random.randint(second_key, (), 0, N_DOM)
    owners = jnp.arange(N_DOM, dtype=jnp.int32)
    extra = jnp.where(owners == full_part, spare, extra)
    extra = jnp.where(owners == (full_part + 1) % N_DOM, 0, extra)
    slot = jnp.arange(TILES_DEV, dtype=jnp.int32)[None, :]
    random_dst = jax.random.randint(third_key, (N_DOM, TILES_DEV), 0, block_count)
    random_src = jax.random.randint(fourth_key, (N_DOM, TILES_DEV), 0, block_count + halo_blocks)
    targets = jnp.where(slot < block_count, slot, random_dst)
    sources = jnp.where(slot < block_count + halo_blocks, slot, random_src)
    live = slot < block_count + halo_blocks + extra[:, None]
    targets = jnp.where(live, targets, -1)
    sources = jnp.where(live, sources, 0)
    return (targets.astype(jnp.int32), sources.astype(jnp.int32))


def draw_tile_dst(key, part):
    return tile_lists(key)[0]


def draw_tile_src(key, part):
    return tile_lists(key)[1]


def draw_features(key, part):
    noise_key, level_key, factor_key, vector_key = jax.random.split(jax.random.fold_in(key, 23), 4)
    shape = (NODE_COUNT, IN_WIDTH)
    noise = jnp.clip(jax.random.normal(noise_key, shape, jnp.float32), -4.0, 4.0)
    levels = jnp.exp(jax.random.uniform(level_key, (N_DOM, 1), jnp.float32, jnp.log(0.3), jnp.log(3.0)))
    factors = jnp.exp(jax.random.uniform(factor_key, (N_DOM, ROWS_DEV), jnp.float32, jnp.log(0.7), 0.0))
    direction = jnp.clip(jax.random.normal(vector_key, (1, IN_WIDTH), jnp.float32), -3.0, 3.0)
    common = (levels * factors).reshape(NODE_COUNT, 1) * direction
    return (noise + common).astype(jnp.bfloat16)


def draw_tiles(key, part):
    block_count = ROWS_DEV // TILE_SIDE
    first_key, second_key, third_key = jax.random.split(jax.random.fold_in(key, 11), 3)
    shape = (N_DOM, TILES_DEV, TILE_SIDE, TILE_SIDE)
    present = (jax.random.randint(first_key, shape, 0, 32) == 0).astype(jnp.float32)
    values = jnp.exp(jax.random.uniform(second_key, shape, jnp.float32, jnp.log(0.001), 0.0))
    selfw = jnp.exp(jax.random.uniform(third_key, (N_DOM, TILES_DEV, 1, TILE_SIDE), jnp.float32, jnp.log(0.1), 0.0))
    diagonal_slot = (jnp.arange(TILES_DEV) < block_count).astype(jnp.float32)[None, :, None, None]
    identity = jnp.eye(TILE_SIDE, dtype=jnp.float32)[None, None, :, :]
    result = present * values + identity * selfw * diagonal_slot
    return result.astype(jnp.bfloat16)


def set_ends(array, stream_key, smallest, largest):
    longest = array.shape.index(max(array.shape))
    spots = []
    for shift in (0, 1):
        where = [jax.random.randint(jax.random.fold_in(stream_key, axis), (), 0, length) for axis, length in enumerate(array.shape)]
        where[longest] = (where[longest] + shift) % array.shape[longest]
        spots.append(tuple(where))
    return array.at[spots[0]].set(smallest).at[spots[1]].set(largest)


def scatter_about(stream_key, shape, width, reach, kind=jnp.bfloat16):
    return jnp.clip(width * jax.random.normal(stream_key, shape, jnp.float32), -reach, reach).astype(kind)


def setup_inputs(seed: int = 0) -> dict:
    keys = jax.random.split(jax.random.key(seed), 9)
    return {
        "features": draw_features(jax.random.fold_in(keys[8], 71), 0),
        "sketch_matrix": scatter_about(keys[1], (IN_WIDTH, SKETCH), IN_WIDTH ** -0.5, 0.21875),
        "tiles": draw_tiles(jax.random.fold_in(keys[8], 71), 0),
        "tile_dst": draw_tile_dst(jax.random.fold_in(keys[8], 71), 0),
        "tile_src": draw_tile_src(jax.random.fold_in(keys[8], 71), 0),
        "halo_index": set_ends(jax.random.randint(keys[5], (N_DOM, HALO_ROWS), 0, ROWS_DEV), jax.random.fold_in(keys[5], 1), 0, ROWS_DEV - 1).astype(jnp.int32),
        "send_order": jax.vmap(lambda own: jax.random.permutation(own, ROWS_DEV))(jax.random.split(keys[6], N_DOM)).reshape((N_DOM, ROWS_DEV)).astype(jnp.int32),
        "arrival_place": jax.vmap(lambda own: jax.random.permutation(own, ROWS_DEV))(jax.random.split(keys[7], N_DOM)).reshape((N_DOM, ROWS_DEV)).astype(jnp.int32),
    }


def propagate(layer, tiles, tile_dst, tile_src, halo_cols, partitions):
    block_count = ROWS_DEV // TILE_SIDE

    def one_part(inputs):
        tile_set, targets, sources, halo_row, index = inputs
        local = lax.dynamic_slice_in_dim(layer, index * ROWS_DEV, ROWS_DEV, 1)
        columns = jnp.concatenate([local, jnp.take(layer, halo_row, axis=1)], 1)
        blocks = columns.reshape(SKETCH, -1, TILE_SIDE)[:, sources, :]
        products = jnp.einsum("ctj,tij->cti", blocks.astype(jnp.float32), tile_set.astype(jnp.float32),
                              precision=lax.Precision.HIGHEST)
        onehot = (targets[:, None] == jnp.arange(block_count, dtype=jnp.int32)[None, :]).astype(jnp.float32)
        summed = jnp.einsum("cti,tb->cbi", products, onehot, precision=lax.Precision.HIGHEST).reshape(SKETCH, ROWS_DEV)
        row_sums = jnp.sum(tile_set, axis=2, dtype=jnp.float32)
        degree = jnp.einsum("ti,tb->bi", row_sums, onehot, precision=lax.Precision.HIGHEST).reshape(ROWS_DEV)
        return (summed / degree[None, :]).astype(jnp.bfloat16)

    result = lax.map(one_part, (tiles, tile_dst, tile_src, halo_cols, partitions))
    return result.transpose(1, 0, 2).reshape(SKETCH, NODE_COUNT)


def reference(features, sketch_matrix, tiles, tile_dst, tile_src, halo_index, send_order, arrival_place):
    hop0 = jnp.dot(features, sketch_matrix, preferred_element_type=jnp.float32).astype(jnp.bfloat16).T
    partitions = jnp.arange(N_DOM, dtype=jnp.int32)
    halo_cols = halo_index.reshape(N_DOM, N_DOM, HALO_SLOT).transpose(1, 0, 2)
    halo_cols = (halo_cols + (partitions * ROWS_DEV)[None, :, None]).reshape(N_DOM, HALO_ROWS).astype(jnp.int32)
    hop1 = propagate(hop0, tiles, tile_dst, tile_src, halo_cols, partitions)
    hop2 = propagate(hop1, tiles, tile_dst, tile_src, halo_cols, partitions)
    source_node = send_order.reshape(N_DOM, N_DOM, LAYOUT_SLOT).transpose(1, 0, 2)
    source_node = (source_node + (partitions * ROWS_DEV)[None, :, None]).reshape(NODE_COUNT).astype(jnp.int32)
    target_node = (arrival_place + (partitions * ROWS_DEV)[:, None]).reshape(NODE_COUNT).astype(jnp.int32)
    stacked = jnp.stack([hop0, hop1, hop2])
    signals = jnp.zeros_like(stacked).at[:, :, target_node].set(stacked[:, :, source_node])
    return signals
```

```python
import jax
import jax.numpy as jnp
from jax import lax
from jax.experimental import pallas as pl
from jax.experimental.pallas import tpu as pltpu
from jax.sharding import PartitionSpec as P

MESH = pl.DeviceIdType.MESH
BF16, F32, I32 = jnp.bfloat16, jnp.float32, jnp.int32
NZ = 8
NA = 16
NREP = 4
CH = 64
NT = 20
HALF = 128

REP, HALO1, HALO2, LAY1, LAY2 = 0, 1, 3, 5, 8


def dot_nt(a, b):
    return lax.dot_general(a, b, (((1,), (1,)), ((), ())), preferred_element_type=F32)


def dot_nn(a, b):
    return lax.dot_general(a, b, (((1,), (0,)), ((), ())), preferred_element_type=F32)


def build(ref, chunk, idx, rows):
    step = 64
    width = idx.shape[1]

    def body(r, _):
        base = pl.multiple_of(r * step, step)
        row = lax.broadcasted_iota(I32, (step, width), 0)
        hot = jnp.where(row == idx - base, 1.0, 0.0).astype(BF16)
        ref[chunk, pl.ds(base, step), :] = hot
        return 0

    lax.fori_loop(0, rows // step, body, 0)


def kernel(
    feat, sketch, tiles, tdst, tsrc, hidx, oidx, pidx, out,
    fbuf, sbuf, tbuf, c0, c1, c2, rs, hs, hr, ub, ts, ls, lr, ls2, arr,
    ohh, ohl, ohp, permh, perml, prods, invd, lsem, ssem, rsem,
):
    dom = lax.axis_index("dom")
    rep = lax.axis_index("rep")
    z = dom // NA
    a = dom % NA
    layers = (c0, c1, c2)

    load_f = pltpu.make_async_copy(feat, fbuf, lsem.at[0])
    load_s = pltpu.make_async_copy(sketch, sbuf, lsem.at[1])
    load_t = pltpu.make_async_copy(tiles, tbuf, lsem.at[2])
    load_s.start()
    load_f.start()
    load_t.start()

    barrier = pltpu.get_barrier_semaphore()

    def greet(o, _):
        pl.semaphore_signal(
            barrier, inc=1, device_id=(z * NA + (a + o) % NA, rep), device_id_type=MESH
        )
        return 0

    def greet_z(o, _):
        pl.semaphore_signal(
            barrier, inc=1, device_id=((z + o) % NZ * NA + a, rep), device_id_type=MESH
        )
        return 0

    def greet_rep(o, _):
        pl.semaphore_signal(
            barrier, inc=1, device_id=(dom, (rep + o) % NREP), device_id_type=MESH
        )
        return 0

    lax.fori_loop(1, NREP, greet_rep, 0)
    lax.fori_loop(1, NA, greet, 0)
    lax.fori_loop(1, NZ, greet_z, 0)

    load_s.wait()
    st = sbuf[...].T
    load_f.wait()
    for h in range(2):
        y = dot_nt(st, fbuf[h * 256 : (h + 1) * 256, :]).astype(BF16)
        for r in range(NREP):
            for k in range(2):
                rs[r, 2 * h + k] = y[r * CH : (r + 1) * CH, k * HALF : (k + 1) * HALF]

    pl.semaphore_wait(barrier, NREP - 1 + NA - 1 + NZ - 1)

    mine = c0.at[pl.ds(rep * 4, 4)]

    def send_rep(o, _):
        to = (rep + o) % NREP
        pltpu.make_async_remote_copy(
            src_ref=rs.at[to], dst_ref=mine, send_sem=ssem.at[REP], recv_sem=rsem.at[REP],
            device_id=(dom, to), device_id_type=MESH,
        ).start()
        return 0

    lax.fori_loop(1, NREP, send_rep, 0)
    pltpu.make_async_copy(rs.at[rep], mine, rsem.at[REP]).start()

    def wait_on(ref, sem):
        pltpu.make_async_copy(ref, ref, sem).wait()

    def send_a(src, dst, row, to):
        @pl.when(to != a)
        def _():
            pltpu.make_async_remote_copy(
                src_ref=src.at[to], dst_ref=dst.at[a], send_sem=ssem.at[row],
                recv_sem=rsem.at[row], device_id=(z * NA + to, rep), device_id_type=MESH,
            ).start()

        @pl.when(to == a)
        def _():
            pltpu.make_async_copy(src.at[to], dst.at[a], rsem.at[row]).start()

    def send_z(src, dst, row, to):
        @pl.when(to != z)
        def _():
            pltpu.make_async_remote_copy(
                src_ref=src.at[to], dst_ref=dst.at[z], send_sem=ssem.at[row],
                recv_sem=rsem.at[row], device_id=(to * NA + a, rep), device_id_type=MESH,
            ).start()

        @pl.when(to == z)
        def _():
            pltpu.make_async_copy(src.at[to], dst.at[z], rsem.at[row]).start()

    def local_cols(c):
        return jnp.concatenate([c[i] for i in range(16)], axis=1)

    low = lax.broadcasted_iota(I32, (32, HALF), 1) < CH

    def halo_start(k):
        c = layers[k]

        def body(i, _):
            chunk = (a // 4 + 2 + i) % 4
            g = dot_nn(local_cols(c), ohh[chunk])
            for p in range(2):
                top = g[0:32, p * HALF : (p + 1) * HALF]
                bot = g[32:64, p * HALF : (p + 1) * HALF]
                hs[k, chunk * 4 + 2 * p] = jnp.where(low, top, pltpu.roll(bot, CH, 1)).astype(BF16)
                hs[k, chunk * 4 + 2 * p + 1] = jnp.where(low, pltpu.roll(top, CH, 1), bot).astype(BF16)
            for j in range(4):
                send_a(hs.at[k], hr.at[k], HALO1 + k, chunk * 4 + j)
            return 0

        lax.fori_loop(0, 4, body, 0)

    def halo_turn(k):
        wait_on(hr.at[k], rsem.at[HALO1 + k])
        for q in range(8):
            r0 = hr[k, 2 * q].astype(F32)
            r1 = hr[k, 2 * q + 1].astype(F32)
            ub[0:32, q * HALF : (q + 1) * HALF] = jnp.where(low, r0, pltpu.roll(r1, CH, 1)).astype(BF16)
            ub[32:64, q * HALF : (q + 1) * HALF] = jnp.where(low, pltpu.roll(r0, CH, 1), r1).astype(BF16)
        dst = layers[k].at[pl.ds(16, NZ)]

        def body(i, _):
            chunk = (z // 2 + 2 + i) % 4
            t = dot_nn(ub[...], permh[chunk]).astype(BF16)
            for p in range(2):
                ts[k, chunk * 2 + p] = t[:, p * HALF : (p + 1) * HALF]
            for p in range(2):
                send_z(ts.at[k], dst, HALO2 + k, chunk * 2 + p)
            return 0

        lax.fori_loop(0, 4, body, 0)

    def layout_start(k):
        c = layers[k]

        def body(i, _):
            chunk = (a // 2 + 4 + i) % 8
            g = dot_nn(local_cols(c), ohl[chunk]).astype(BF16)
            for p in range(2):
                ls[k, chunk * 2 + p] = g[:, p * HALF : (p + 1) * HALF]
            for p in range(2):
                send_a(ls.at[k], lr.at[k], LAY1 + k, chunk * 2 + p)
            return 0

        lax.fori_loop(0, 8, body, 0)

    def layout_turn(k):
        wait_on(lr.at[k], rsem.at[LAY1 + k])

        def body(i, _):
            chunk = (z // 2 + 2 + i) % 4
            x = jnp.concatenate(
                [jnp.concatenate([lr[k, g * 8 + j] for j in range(8)], axis=1) for g in range(2)],
                axis=0,
            )
            t = dot_nn(x, perml[chunk]).astype(BF16)
            for p in range(2):
                for g in range(2):
                    ls2[k, chunk * 2 + p, g] = t[g * CH : (g + 1) * CH, p * HALF : (p + 1) * HALF]
            for p in range(2):
                send_z(ls2.at[k], arr.at[k], LAY2 + k, chunk * 2 + p)
            return 0

        lax.fori_loop(0, 4, body, 0)

    def product(c, t, s):
        x = jnp.concatenate([c[2 * s], c[2 * s + 1]], axis=1)
        prods[t] = dot_nt(x, tbuf[t])

    def combine_local(k):
        def body(t, _):
            product(layers[k], t, t)
            return 0

        lax.fori_loop(0, 8, body, 0)

    def mask(t, b):
        return jnp.where(tdst[0, t] == b, 1.0, 0.0).astype(F32)

    def combine_rest(k):
        wait_on(layers[k].at[pl.ds(16, NZ)], rsem.at[HALO2 + k])

        def body(t, _):
            product(layers[k], t, tsrc[0, t])
            return 0

        lax.fori_loop(8, NT, body, 0)
        nxt = layers[k + 1]

        def total(b, _):
            acc = prods[b]
            for t in range(8, NT):
                acc += mask(t, b) * prods[t]
            hop = (acc * invd[b][0:1, :]).astype(BF16)
            nxt[2 * b] = hop[:, :HALF]
            nxt[2 * b + 1] = hop[:, HALF:]
            return 0

        lax.fori_loop(0, 8, total, 0)

    def build_h(i, _):
        build(ohh, i, hidx[pl.ds(i, 1), :], 2048)
        return 0

    lax.fori_loop(0, 4, build_h, 0)
    load_t.wait()

    def row_sums(t, _):
        prods[t, 0:16, :] = dot_nt(jnp.ones((16, 256), BF16), tbuf[t])
        return 0

    lax.fori_loop(0, NT, row_sums, 0)

    def degrees(b, _):
        acc = prods[b, 0:8, :]
        for t in range(8, NT):
            acc += mask(t, b) * prods[t, 0:8, :]
        invd[b] = 1.0 / acc
        return 0

    lax.fori_loop(0, 8, degrees, 0)

    def build_ph(i, _):
        m = lax.broadcasted_iota(I32, (1, 256), 1) + i * 256
        build(permh, i, ((m >> 3) & 15) * 64 + (m >> 7) * 8 + (m & 7), 1024)
        return 0

    lax.fori_loop(0, 4, build_ph, 0)

    wait_on(c0.at[pl.ds(0, 16)], rsem.at[REP])
    halo_start(0)

    def build_l(i, _):
        build(ohl, i, oidx[pl.ds(i, 1), :], 2048)
        return 0

    lax.fori_loop(0, 8, build_l, 0)
    halo_turn(0)
    layout_start(0)
    combine_local(0)

    def build_pl(i, _):
        m = lax.broadcasted_iota(I32, (1, 256), 1) + i * 256
        build(perml, i, ((m >> 4) & 7) * 128 + (m >> 7) * 16 + (m & 15), 1024)
        return 0

    lax.fori_loop(0, 4, build_pl, 0)
    combine_rest(0)
    halo_start(1)
    layout_turn(0)
    halo_turn(1)
    layout_start(1)
    combine_local(1)

    def build_p(i, _):
        build(ohp, i, pidx[...] - i * 256, 256)
        return 0

    lax.fori_loop(0, 8, build_p, 0)
    combine_rest(1)
    layout_start(2)
    layout_turn(1)
    layout_turn(2)

    for k in range(3):
        wait_on(arr.at[k], rsem.at[LAY2 + k])

    def place(j, _):
        acc = jnp.zeros((3 * CH, 256), F32)
        for zz in range(NZ):
            x = jnp.concatenate(
                [jnp.concatenate([arr[k, zz, 0], arr[k, zz, 1]], axis=1) for k in range(3)], axis=0
            )
            acc += dot_nt(x, ohp[j, :, zz * 256 : (zz + 1) * 256])
        res = acc.astype(BF16)
        for k in range(3):
            out[k, :, pl.ds(pl.multiple_of(j * 256, 256), 256)] = res[k * CH : (k + 1) * CH]
        return 0

    lax.fori_loop(0, 8, place, 0)

    wait_on(rs.at[pl.ds(0, NREP - 1)], ssem.at[REP])
    for k in range(2):
        wait_on(hs.at[k, pl.ds(0, NA - 1)], ssem.at[HALO1 + k])
        wait_on(ts.at[k, pl.ds(0, NZ - 1)], ssem.at[HALO2 + k])
    for k in range(3):
        wait_on(ls.at[k, pl.ds(0, NA - 1)], ssem.at[LAY1 + k])
        wait_on(ls2.at[k, pl.ds(0, NZ - 1)], ssem.at[LAY2 + k])


def on_device(features, sketch_matrix, tiles, tile_dst, tile_src, halo_index, send_order, arrival_place):
    hidx = halo_index.reshape(NZ, NA, 8).transpose(1, 0, 2).reshape(4, 256)
    oidx = send_order.reshape(NZ, NA, 16).transpose(1, 0, 2).reshape(8, 256)
    vm, sm, hbm = (pl.BlockSpec(memory_space=s) for s in (pltpu.VMEM, pltpu.SMEM, pl.ANY))
    return pl.pallas_call(
        kernel,
        out_shape=jax.ShapeDtypeStruct((3, CH, 2048), BF16),
        in_specs=[hbm, hbm, hbm, sm, sm, vm, vm, vm],
        out_specs=vm,
        scratch_shapes=[
            pltpu.VMEM((512, 768), BF16),
            pltpu.VMEM((768, 256), BF16),
            pltpu.VMEM((NT, 256, 256), BF16),
            pltpu.VMEM((24, CH, HALF), BF16),
            pltpu.VMEM((24, CH, HALF), BF16),
            pltpu.VMEM((16, CH, HALF), BF16),
            pltpu.VMEM((NREP, 4, CH, HALF), BF16),
            pltpu.VMEM((2, NA, 32, HALF), BF16),
            pltpu.VMEM((2, NA, 32, HALF), BF16),
            pltpu.VMEM((CH, 1024), BF16),
            pltpu.VMEM((2, NZ, CH, HALF), BF16),
            pltpu.VMEM((3, NA, CH, HALF), BF16),
            pltpu.VMEM((3, NA, CH, HALF), BF16),
            pltpu.VMEM((3, NZ, 2, CH, HALF), BF16),
            pltpu.VMEM((3, NZ, 2, CH, HALF), BF16),
            pltpu.VMEM((4, 2048, 256), BF16),
            pltpu.VMEM((8, 2048, 256), BF16),
            pltpu.VMEM((8, 256, 2048), BF16),
            pltpu.VMEM((4, 1024, 256), BF16),
            pltpu.VMEM((4, 1024, 256), BF16),
            pltpu.VMEM((NT, CH, 256), F32),
            pltpu.VMEM((8, 8, 256), F32),
            pltpu.SemaphoreType.DMA((3,)),
            pltpu.SemaphoreType.DMA((11,)),
            pltpu.SemaphoreType.DMA((11,)),
        ],
        compiler_params=pltpu.CompilerParams(
            collective_id=0, has_side_effects=True, vmem_limit_bytes=56 * 2**20
        ),
    )(features, sketch_matrix, tiles[0], tile_dst, tile_src, hidx, oidx, arrival_place)


def solution(mesh):
    in_specs = (
        P(("dom", "rep"), None),
        P(),
        P("dom", None, None, None),
        P("dom", None),
        P("dom", None),
        P("dom", None),
        P("dom", None),
        P("dom", None),
    )
    return jax.shard_map(
        on_device, mesh=mesh, in_specs=in_specs, out_specs=P(None, "rep", "dom"), check_vma=False
    )
```

```python
import jax
import jax.numpy as jnp
from jax import lax
from jax.experimental import pallas as pl
from jax.experimental.pallas import tpu as pltpu
from jax.sharding import PartitionSpec as P

MESH = pl.DeviceIdType.MESH
BF16, F32, I32 = jnp.bfloat16, jnp.float32, jnp.int32
NZ = 8
NA = 16
NREP = 4
CH = 64
NT = 20
HALF = 128

REP, HALO1, HALO2, LAY1, LAY2, LAST = 0, 1, 3, 5, 8, 11


def dot_nt(a, b):
    return lax.dot_general(a, b, (((1,), (1,)), ((), ())), preferred_element_type=F32)


def dot_nn(a, b):
    return lax.dot_general(a, b, (((1,), (0,)), ((), ())), preferred_element_type=F32)


def build(ref, chunk, idx, rows):
    step = 64
    width = idx.shape[1]

    def body(r, _):
        base = pl.multiple_of(r * step, step)
        row = lax.broadcasted_iota(I32, (step, width), 0)
        hot = jnp.where(row == idx - base, 1.0, 0.0).astype(BF16)
        ref[chunk, pl.ds(base, step), :] = hot
        return 0

    lax.fori_loop(0, rows // step, body, 0)


def far_first(i):
    return jnp.where(i == 0, 2, jnp.where(i == 1, 1, jnp.where(i == 2, 3, 0)))


def regroup(row, picks, width):
    lane = lax.broadcasted_iota(I32, (1, HALF), 1)
    out = jnp.zeros((1, HALF), I32)
    for j, start in enumerate(picks):
        base = start // HALF * HALF
        piece = pltpu.roll(row[:, base : base + HALF], (j * width - (start - base)) % HALF, 1)
        out = jnp.where(lane // width == j, piece, out)
    return out


def permute(x, perm):
    return sum(dot_nt(x[:, c * 256 : (c + 1) * 256], perm[c]) for c in range(4))


def halves(idx, first, second, row):
    hi, lo = (idx >> 3).astype(F32), (idx & 7).astype(F32)
    return jnp.where(row == first, hi, jnp.where(row == second, lo, 0.0))


def kernel(
    feat, sketch, tiles, tdst, tsrc, hidx, oidx, pidx, out,
    fbuf, sbuf, tbuf, c0, c1, c2, rs, hs, hr, ub, ts, ls, lr, ls2, arr,
    ohh, ohl, ohp, permh, perml, hix, oix, pix, prods, total2, invd, lsem, ssem, rsem,
):
    dom = lax.axis_index("dom")
    rep = lax.axis_index("rep")
    z = dom // NA
    a = dom % NA
    y = a // 2
    core = a % 2
    w = jnp.where(core == 0, z, y)
    layers = (c0, c1, c2)

    load_f = pltpu.make_async_copy(feat, fbuf, lsem.at[0])
    load_s = pltpu.make_async_copy(sketch, sbuf, lsem.at[1])
    load_t = pltpu.make_async_copy(tiles, tbuf, lsem.at[2])
    load_s.start()
    load_f.start()
    load_t.start()

    barrier = pltpu.get_barrier_semaphore()

    def greet(o, _):
        pl.semaphore_signal(
            barrier, inc=1, device_id=(z * NA + (a + o) % NA, rep), device_id_type=MESH
        )
        return 0

    def greet_z(o, _):
        for i in range(2):
            pl.semaphore_signal(
                barrier, inc=1, device_id=((z + o) % NZ * NA + y * 2 + i, rep), device_id_type=MESH
            )
        return 0

    def greet_rep(o, _):
        pl.semaphore_signal(
            barrier, inc=1, device_id=(dom, (rep + o) % NREP), device_id_type=MESH
        )
        return 0

    lax.fori_loop(1, NREP, greet_rep, 0)
    lax.fori_loop(1, NA, greet, 0)
    lax.fori_loop(1, NZ, greet_z, 0)

    def build_ph(i, _):
        m = lax.broadcasted_iota(I32, (1, 256), 1) + i * 256
        build(permh, i, ((m >> 3) & 15) * 64 + (m >> 7) * 8 + (m & 7), 1024)
        return 0

    lax.fori_loop(0, 4, build_ph, 0)

    row16 = lax.broadcasted_iota(I32, (16, 1024), 0)
    h = permute(halves(hidx[...], 0, 1, row16).astype(BF16), permh)
    hp = (h[0:1] * 8.0 + h[1:2]).astype(I32)
    for i in range(4):
        hix[i : i + 1, :] = hp[:, i * 256 : (i + 1) * 256]

    load_s.wait()
    st = sbuf[...].T
    load_f.wait()
    for h in range(2):
        hop = dot_nt(st, fbuf[h * 256 : (h + 1) * 256, :]).astype(BF16)
        for r in range(NREP):
            for k in range(2):
                rs[r, 2 * h + k] = hop[r * CH : (r + 1) * CH, k * HALF : (k + 1) * HALF]

    pl.semaphore_wait(barrier, NREP - 1 + NA - 1 + 2 * (NZ - 1))

    mine = c0.at[pl.ds(rep * 4, 4)]

    def send_rep(o, _):
        to = (rep + jnp.where(o == 1, 2, jnp.where(o == 2, 1, 3))) % NREP
        pltpu.make_async_remote_copy(
            src_ref=rs.at[to], dst_ref=mine, send_sem=ssem.at[REP], recv_sem=rsem.at[REP],
            device_id=(dom, to), device_id_type=MESH,
        ).start()
        return 0

    lax.fori_loop(1, NREP, send_rep, 0)
    pltpu.make_async_copy(rs.at[rep], mine, rsem.at[REP]).start()

    def wait_on(ref, sem):
        pltpu.make_async_copy(ref, ref, sem).wait()

    def send_a(src, dst, row, to):
        @pl.when(to != a)
        def _():
            pltpu.make_async_remote_copy(
                src_ref=src.at[to], dst_ref=dst.at[a], send_sem=ssem.at[row],
                recv_sem=rsem.at[row], device_id=(z * NA + to, rep), device_id_type=MESH,
            ).start()

        @pl.when(to == a)
        def _():
            pltpu.make_async_copy(src.at[to], dst.at[a], rsem.at[row]).start()

    def send_z(src, dst, row, to):
        @pl.when(to != z)
        def _():
            pltpu.make_async_remote_copy(
                src_ref=src.at[to], dst_ref=dst.at[z], send_sem=ssem.at[row],
                recv_sem=rsem.at[row], device_id=(to * NA + a, rep), device_id_type=MESH,
            ).start()

        @pl.when(to == z)
        def _():
            pltpu.make_async_copy(src.at[to], dst.at[z], rsem.at[row]).start()

    def send_first(k, m):
        to = jnp.where(m < 8, z * NA + m * 2, (m - 8) * NA + y * 2 + 1)
        slot = jnp.where(m < 8, a, z * 2 + core)
        row = LAY1 + k

        @pl.when(to != dom)
        def _():
            pltpu.make_async_remote_copy(
                src_ref=ls.at[k, m], dst_ref=lr.at[k, slot], send_sem=ssem.at[row],
                recv_sem=rsem.at[row], device_id=(to, rep), device_id_type=MESH,
            ).start()

        @pl.when(to == dom)
        def _():
            pltpu.make_async_copy(ls.at[k, m], lr.at[k, slot], rsem.at[row]).start()

    def send_second(k, m):
        to = jnp.where(core == 0, m * NA + a, z * NA + m * 2 + 1)
        got = rsem.at[LAST + w] if k == 2 else rsem.at[LAY2 + k]

        @pl.when(m != w)
        def _():
            pltpu.make_async_remote_copy(
                src_ref=ls2.at[k, m], dst_ref=arr.at[k, w], send_sem=ssem.at[LAY2 + k],
                recv_sem=got, device_id=(to, rep), device_id_type=MESH,
            ).start()

        @pl.when(m == w)
        def _():
            pltpu.make_async_copy(ls2.at[k, m], arr.at[k, w], got).start()

    def local_cols(c):
        return jnp.concatenate([c[i] for i in range(16)], axis=1)

    low = lax.broadcasted_iota(I32, (32, HALF), 1) < CH

    def halo_start(k):
        c = layers[k]

        def body(i, _):
            chunk = (a // 4 + far_first(i)) % 4
            g = dot_nn(local_cols(c), ohh[chunk])
            for p in range(2):
                top = g[0:32, p * HALF : (p + 1) * HALF]
                bot = g[32:64, p * HALF : (p + 1) * HALF]
                hs[k, chunk * 4 + 2 * p] = jnp.where(low, top, pltpu.roll(bot, CH, 1)).astype(BF16)
                hs[k, chunk * 4 + 2 * p + 1] = jnp.where(low, pltpu.roll(top, CH, 1), bot).astype(BF16)
            for j in range(4):
                send_a(hs.at[k], hr.at[k], HALO1 + k, chunk * 4 + j)
            return 0

        lax.fori_loop(0, 4, body, 0)

    def halo_turn(k):
        wait_on(hr.at[k], rsem.at[HALO1 + k])
        for q in range(8):
            r0 = hr[k, 2 * q].astype(F32)
            r1 = hr[k, 2 * q + 1].astype(F32)
            ub[0:32, q * HALF : (q + 1) * HALF] = jnp.where(low, r0, pltpu.roll(r1, CH, 1)).astype(BF16)
            ub[32:64, q * HALF : (q + 1) * HALF] = jnp.where(low, pltpu.roll(r0, CH, 1), r1).astype(BF16)
        dst = layers[k].at[pl.ds(16, NZ)]

        def body(i, _):
            chunk = (z // 2 + far_first(i)) % 4
            t = dot_nn(ub[...], permh[chunk]).astype(BF16)
            for p in range(2):
                ts[k, chunk * 2 + p] = t[:, p * HALF : (p + 1) * HALF]
            for p in range(2):
                send_z(ts.at[k], dst, HALO2 + k, chunk * 2 + p)
            return 0

        lax.fori_loop(0, 4, body, 0)

    def layout_start(k):
        c = layers[k]

        def body(i, _):
            off = far_first(i // 2)
            chunk = jnp.where(i % 2 == 0, (y // 2 + off) % 4, 4 + (z // 2 + off) % 4)
            g = dot_nn(local_cols(c), ohl[chunk]).astype(BF16)
            for p in range(2):
                ls[k, chunk * 2 + p] = g[:, p * HALF : (p + 1) * HALF]
            for p in range(2):
                send_first(k, chunk * 2 + p)
            return 0

        lax.fori_loop(0, 8, body, 0)

    def layout_turn(k):
        wait_on(lr.at[k], rsem.at[LAY1 + k])

        def body(i, _):
            chunk = (w // 2 + far_first(i)) % 4
            x = jnp.concatenate(
                [jnp.concatenate([lr[k, g * 8 + j] for j in range(8)], axis=1) for g in range(2)],
                axis=0,
            )
            t = dot_nn(x, perml[chunk]).astype(BF16)
            for p in range(2):
                for g in range(2):
                    ls2[k, chunk * 2 + p, g] = t[g * CH : (g + 1) * CH, p * HALF : (p + 1) * HALF]
            for p in range(2):
                send_second(k, chunk * 2 + p)
            return 0

        lax.fori_loop(0, 4, body, 0)

    def product(c, t, s):
        x = jnp.concatenate([c[2 * s], c[2 * s + 1]], axis=1)
        prods[t] = dot_nt(x, tbuf[t])

    def combine_local(k):
        def body(i, _):
            for j in range(4):
                product(layers[k], i * 4 + j, i * 4 + j)
            return 0

        lax.fori_loop(0, 2, body, 0)

    def mask(t, b):
        return jnp.where(tdst[0, t] == b, 1.0, 0.0).astype(F32)

    def combine_rest(k):
        wait_on(layers[k].at[pl.ds(16, NZ)], rsem.at[HALO2 + k])

        def body(i, _):
            for j in range(4):
                product(layers[k], i * 4 + j, tsrc[0, i * 4 + j])
            return 0

        lax.fori_loop(2, 5, body, 0)
        nxt = layers[k + 1]

        def total(b, _):
            acc = prods[b]
            for t in range(8, NT):
                acc += mask(t, b) * prods[t]
            hop = (acc * invd[b][0:1, :]).astype(BF16)
            nxt[2 * b] = hop[:, :HALF]
            nxt[2 * b + 1] = hop[:, HALF:]
            return 0

        lax.fori_loop(0, 8, total, 0)

    def build_h(i, _):
        build(ohh, i, hix[pl.ds(i, 1), :], 2048)
        return 0

    lax.fori_loop(0, 4, build_h, 0)

    def build_pl(i, _):
        m = lax.broadcasted_iota(I32, (1, 256), 1) + i * 256
        build(perml, i, ((m >> 4) & 7) * 128 + (m >> 7) * 16 + (m & 15), 1024)
        return 0

    lax.fori_loop(0, 4, build_pl, 0)
    order = oidx[...]
    for m in range(16):
        if m < 8:
            picks = [j * 256 + m * 32 for j in range(8)]
        else:
            picks = [(m - 8) * 256 + j * 32 + 16 for j in range(8)]
        oix[m // 2 : m // 2 + 1, m % 2 * HALF : (m % 2 + 1) * HALF] = regroup(order, picks, 16)

    wait_on(c0.at[pl.ds(0, 16)], rsem.at[REP])
    halo_start(0)

    def build_l(i, _):
        build(ohl, i, oix[pl.ds(i, 1), :], 2048)
        return 0

    lax.fori_loop(0, 8, build_l, 0)
    layout_start(0)
    halo_turn(0)
    load_t.wait()

    def row_sums(i, _):
        for j in range(4):
            prods[i * 4 + j, 0:16, :] = dot_nt(jnp.ones((16, 256), BF16), tbuf[i * 4 + j])
        return 0

    lax.fori_loop(0, 5, row_sums, 0)

    def degrees(b, _):
        acc = prods[b, 0:8, :]
        for t in range(8, NT):
            acc += mask(t, b) * prods[t, 0:8, :]
        invd[b] = 1.0 / acc
        return 0

    lax.fori_loop(0, 8, degrees, 0)
    combine_local(0)

    nat = pidx[...]
    for m in range(16):
        own = nat[:, m * HALF : (m + 1) * HALF]
        picks = [(m % 2 * 4 + j) * 256 + m // 2 * 32 for j in range(4)]
        turned = regroup(nat, picks, 32)
        pix[m // 2 : m // 2 + 1, m % 2 * HALF : (m % 2 + 1) * HALF] = jnp.where(core == 0, own, turned)

    def build_p(i, _):
        build(ohp, i, pix[pl.ds(i, 1), :], 2048)
        return 0

    lax.fori_loop(0, 8, build_p, 0)
    combine_rest(0)
    halo_start(1)
    layout_turn(0)
    layout_start(1)
    halo_turn(1)
    combine_local(1)
    layout_turn(1)
    combine_rest(1)
    layout_start(2)

    def arrived(k, m):
        return jnp.concatenate([arr[k, m, 0], arr[k, m, 1]], axis=1)

    for k in range(2):
        wait_on(arr.at[k], rsem.at[LAY2 + k])

    def place(j, _):
        rows = pl.ds(pl.multiple_of(j * 256, 256), 256)
        acc = jnp.zeros((2 * CH, 256), F32)
        for m in range(NZ):
            x = jnp.concatenate([arrived(0, m), arrived(1, m)], axis=0)
            acc += dot_nt(x, ohp[m, rows, :])
        res = acc.astype(BF16)
        for k in range(2):
            out[k, :, rows] = res[k * CH : (k + 1) * CH]
        return 0

    lax.fori_loop(0, 8, place, 0)
    layout_turn(2)
    total2[...] = jnp.zeros((CH, 2048), F32)

    def place_last(i, _):
        step = (i + 1) // 2
        m = (w + jnp.where(i % 2 == 0, step, NZ - step)) % NZ
        wait_on(arr.at[2, m], rsem.at[LAST + m])
        total2[...] += dot_nt(arrived(2, m), ohp[m])
        return 0

    lax.fori_loop(0, NZ, place_last, 0)
    out[2] = total2[...].astype(BF16)

    wait_on(rs.at[pl.ds(0, NREP - 1)], ssem.at[REP])
    for k in range(2):
        wait_on(hs.at[k, pl.ds(0, NA - 1)], ssem.at[HALO1 + k])
        wait_on(ts.at[k, pl.ds(0, NZ - 1)], ssem.at[HALO2 + k])
    for k in range(3):
        wait_on(ls.at[k, pl.ds(0, NA - 1)], ssem.at[LAY1 + k])
        wait_on(ls2.at[k, pl.ds(0, NZ - 1)], ssem.at[LAY2 + k])


def on_device(features, sketch_matrix, tiles, tile_dst, tile_src, halo_index, send_order, arrival_place):
    vm, sm, hbm = (pl.BlockSpec(memory_space=s) for s in (pltpu.VMEM, pltpu.SMEM, pl.ANY))
    return pl.pallas_call(
        kernel,
        out_shape=jax.ShapeDtypeStruct((3, CH, 2048), BF16),
        in_specs=[hbm, hbm, hbm, sm, sm, vm, vm, vm],
        out_specs=vm,
        scratch_shapes=[
            pltpu.VMEM((512, 768), BF16),
            pltpu.VMEM((768, 256), BF16),
            pltpu.VMEM((NT, 256, 256), BF16),
            pltpu.VMEM((24, CH, HALF), BF16),
            pltpu.VMEM((24, CH, HALF), BF16),
            pltpu.VMEM((16, CH, HALF), BF16),
            pltpu.VMEM((NREP, 4, CH, HALF), BF16),
            pltpu.VMEM((2, NA, 32, HALF), BF16),
            pltpu.VMEM((2, NA, 32, HALF), BF16),
            pltpu.VMEM((CH, 1024), BF16),
            pltpu.VMEM((2, NZ, CH, HALF), BF16),
            pltpu.VMEM((3, NA, CH, HALF), BF16),
            pltpu.VMEM((3, NA, CH, HALF), BF16),
            pltpu.VMEM((3, NZ, 2, CH, HALF), BF16),
            pltpu.VMEM((3, NZ, 2, CH, HALF), BF16),
            pltpu.VMEM((4, 2048, 256), BF16),
            pltpu.VMEM((8, 2048, 256), BF16),
            pltpu.VMEM((8, 2048, 256), BF16),
            pltpu.VMEM((4, 1024, 256), BF16),
            pltpu.VMEM((4, 1024, 256), BF16),
            pltpu.VMEM((4, 256), I32),
            pltpu.VMEM((8, 256), I32),
            pltpu.VMEM((8, 256), I32),
            pltpu.VMEM((NT, CH, 256), F32),
            pltpu.VMEM((CH, 2048), F32),
            pltpu.VMEM((8, 8, 256), F32),
            pltpu.SemaphoreType.DMA((3,)),
            pltpu.SemaphoreType.DMA((11,)),
            pltpu.SemaphoreType.DMA((19,)),
        ],
        compiler_params=pltpu.CompilerParams(
            collective_id=0, has_side_effects=True, vmem_limit_bytes=56 * 2**20
        ),
    )(features, sketch_matrix, tiles[0], tile_dst, tile_src, halo_index, send_order, arrival_place)


def solution(mesh):
    in_specs = (
        P(("dom", "rep"), None),
        P(),
        P("dom", None, None, None),
        P("dom", None),
        P("dom", None),
        P("dom", None),
        P("dom", None),
        P("dom", None),
    )
    return jax.shard_map(
        on_device, mesh=mesh, in_specs=in_specs, out_specs=P(None, "rep", "dom"), check_vma=False
    )
```

```python
import jax
import jax.numpy as jnp
from jax import lax
from jax.experimental import pallas as pl
from jax.experimental.pallas import tpu as pltpu
from jax.sharding import PartitionSpec as P

MESH = pl.DeviceIdType.MESH
BF16, F32, I32 = jnp.bfloat16, jnp.float32, jnp.int32
NZ = 8
NA = 16
NREP = 4
CH = 64
NT = 20
HALF = 128

REP, HALO1, HALO2, LAY1, LAY2, LAST = 0, 1, 3, 5, 8, 11


def dot_nt(a, b):
    return lax.dot_general(a, b, (((1,), (1,)), ((), ())), preferred_element_type=F32)


def dot_nn(a, b):
    return lax.dot_general(a, b, (((1,), (0,)), ((), ())), preferred_element_type=F32)


def build(ref, chunk, idx, rows):
    step = 64
    width = idx.shape[1]

    def body(r, _):
        base = pl.multiple_of(r * step, step)
        row = lax.broadcasted_iota(I32, (step, width), 0)
        hot = jnp.where(row == idx - base, 1.0, 0.0).astype(BF16)
        ref[chunk, pl.ds(base, step), :] = hot
        return 0

    lax.fori_loop(0, rows // step, body, 0)


def far_first(i):
    return jnp.where(i == 0, 2, jnp.where(i == 1, 1, jnp.where(i == 2, 3, 0)))


def regroup(row, picks, width):
    lane = lax.broadcasted_iota(I32, (1, HALF), 1)
    out = jnp.zeros((1, HALF), I32)
    for j, start in enumerate(picks):
        base = start // HALF * HALF
        piece = pltpu.roll(row[:, base : base + HALF], (j * width - (start - base)) % HALF, 1)
        out = jnp.where(lane // width == j, piece, out)
    return out


def permute(x, perm):
    return sum(dot_nt(x[:, c * 256 : (c + 1) * 256], perm[c]) for c in range(4))


def halves(idx, first, second, row):
    hi, lo = (idx >> 3).astype(F32), (idx & 7).astype(F32)
    return jnp.where(row == first, hi, jnp.where(row == second, lo, 0.0))


def kernel(
    feat, sketch, tiles, tdst, tsrc, hidx, oidx, pidx, out,
    fbuf, sbuf, tbuf, c0, c1, c2, rs, hs, hr, ub, ts, ls, lr, ls2, arr,
    ohh, ohl, ohp, permh, perml, hix, oix, pix, prods, total2, invd, lsem, ssem, rsem,
):
    dom = lax.axis_index("dom")
    rep = lax.axis_index("rep")
    z = dom // NA
    a = dom % NA
    y = a // 2
    core = a % 2
    w = jnp.where(core == 0, z, y)
    layers = (c0, c1, c2)

    load_f = pltpu.make_async_copy(feat, fbuf, lsem.at[0])
    load_s = pltpu.make_async_copy(sketch, sbuf, lsem.at[1])
    load_t = pltpu.make_async_copy(tiles, tbuf, lsem.at[2])
    load_s.start()
    load_f.start()
    load_t.start()

    barrier = pltpu.get_barrier_semaphore()

    def greet(o, _):
        pl.semaphore_signal(
            barrier, inc=1, device_id=(z * NA + (a + o) % NA, rep), device_id_type=MESH
        )
        return 0

    def greet_z(o, _):
        for i in range(2):
            pl.semaphore_signal(
                barrier, inc=1, device_id=((z + o) % NZ * NA + y * 2 + i, rep), device_id_type=MESH
            )
        return 0

    def greet_rep(o, _):
        pl.semaphore_signal(
            barrier, inc=1, device_id=(dom, (rep + o) % NREP), device_id_type=MESH
        )
        return 0

    lax.fori_loop(1, NREP, greet_rep, 0)
    lax.fori_loop(1, NA, greet, 0)
    lax.fori_loop(1, NZ, greet_z, 0)

    load_s.wait()
    st = sbuf[...].T
    load_f.wait()
    for h in range(2):
        hop = dot_nt(st, fbuf[h * 256 : (h + 1) * 256, :]).astype(BF16)
        for r in range(NREP):
            for k in range(2):
                rs[r, 2 * h + k] = hop[r * CH : (r + 1) * CH, k * HALF : (k + 1) * HALF]

    pl.semaphore_wait(barrier, NREP - 1 + NA - 1 + 2 * (NZ - 1))

    mine = c0.at[pl.ds(rep * 4, 4)]

    def send_rep(o, _):
        to = (rep + jnp.where(o == 1, 2, jnp.where(o == 2, 1, 3))) % NREP
        pltpu.make_async_remote_copy(
            src_ref=rs.at[to], dst_ref=mine, send_sem=ssem.at[REP], recv_sem=rsem.at[REP],
            device_id=(dom, to), device_id_type=MESH,
        ).start()
        return 0

    lax.fori_loop(1, NREP, send_rep, 0)
    pltpu.make_async_copy(rs.at[rep], mine, rsem.at[REP]).start()

    def wait_on(ref, sem):
        pltpu.make_async_copy(ref, ref, sem).wait()

    def send_a(src, dst, row, to):
        @pl.when(to != a)
        def _():
            pltpu.make_async_remote_copy(
                src_ref=src.at[to], dst_ref=dst.at[a], send_sem=ssem.at[row],
                recv_sem=rsem.at[row], device_id=(z * NA + to, rep), device_id_type=MESH,
            ).start()

        @pl.when(to == a)
        def _():
            pltpu.make_async_copy(src.at[to], dst.at[a], rsem.at[row]).start()

    def send_z(src, dst, row, to):
        @pl.when(to != z)
        def _():
            pltpu.make_async_remote_copy(
                src_ref=src.at[to], dst_ref=dst.at[z], send_sem=ssem.at[row],
                recv_sem=rsem.at[row], device_id=(to * NA + a, rep), device_id_type=MESH,
            ).start()

        @pl.when(to == z)
        def _():
            pltpu.make_async_copy(src.at[to], dst.at[z], rsem.at[row]).start()

    def send_first(k, m):
        to = jnp.where(m < 8, z * NA + m * 2, (m - 8) * NA + y * 2 + 1)
        slot = jnp.where(m < 8, a, z * 2 + core)
        row = LAY1 + k

        @pl.when(to != dom)
        def _():
            pltpu.make_async_remote_copy(
                src_ref=ls.at[k, m], dst_ref=lr.at[k, slot], send_sem=ssem.at[row],
                recv_sem=rsem.at[row], device_id=(to, rep), device_id_type=MESH,
            ).start()

        @pl.when(to == dom)
        def _():
            pltpu.make_async_copy(ls.at[k, m], lr.at[k, slot], rsem.at[row]).start()

    def send_second(k, m):
        to = jnp.where(core == 0, m * NA + a, z * NA + m * 2 + 1)
        got = rsem.at[LAST + w] if k == 2 else rsem.at[LAY2 + k]

        @pl.when(m != w)
        def _():
            pltpu.make_async_remote_copy(
                src_ref=ls2.at[k, m], dst_ref=arr.at[k, w], send_sem=ssem.at[LAY2 + k],
                recv_sem=got, device_id=(to, rep), device_id_type=MESH,
            ).start()

        @pl.when(m == w)
        def _():
            pltpu.make_async_copy(ls2.at[k, m], arr.at[k, w], got).start()

    def local_cols(c):
        return jnp.concatenate([c[i] for i in range(16)], axis=1)

    low = lax.broadcasted_iota(I32, (32, HALF), 1) < CH

    def halo_start(k):
        c = layers[k]

        def body(i, _):
            chunk = (a // 4 + far_first(i)) % 4
            g = dot_nn(local_cols(c), ohh[chunk])
            for p in range(2):
                top = g[0:32, p * HALF : (p + 1) * HALF]
                bot = g[32:64, p * HALF : (p + 1) * HALF]
                hs[k, chunk * 4 + 2 * p] = jnp.where(low, top, pltpu.roll(bot, CH, 1)).astype(BF16)
                hs[k, chunk * 4 + 2 * p + 1] = jnp.where(low, pltpu.roll(top, CH, 1), bot).astype(BF16)
            for j in range(4):
                send_a(hs.at[k], hr.at[k], HALO1 + k, chunk * 4 + j)
            return 0

        lax.fori_loop(0, 4, body, 0)

    def halo_turn(k):
        wait_on(hr.at[k], rsem.at[HALO1 + k])
        for q in range(8):
            r0 = hr[k, 2 * q].astype(F32)
            r1 = hr[k, 2 * q + 1].astype(F32)
            ub[0:32, q * HALF : (q + 1) * HALF] = jnp.where(low, r0, pltpu.roll(r1, CH, 1)).astype(BF16)
            ub[32:64, q * HALF : (q + 1) * HALF] = jnp.where(low, pltpu.roll(r0, CH, 1), r1).astype(BF16)
        dst = layers[k].at[pl.ds(16, NZ)]

        def body(i, _):
            chunk = (z // 2 + far_first(i)) % 4
            t = dot_nn(ub[...], permh[chunk]).astype(BF16)
            for p in range(2):
                ts[k, chunk * 2 + p] = t[:, p * HALF : (p + 1) * HALF]
            for p in range(2):
                send_z(ts.at[k], dst, HALO2 + k, chunk * 2 + p)
            return 0

        lax.fori_loop(0, 4, body, 0)

    def layout_start(k, only=None):
        c = layers[k]

        def body(i, _):
            off = far_first(i // 2 if only is None else i)
            over_y = i % 2 == 0 if only is None else only == "y"
            chunk = jnp.where(over_y, (y // 2 + off) % 4, 4 + (z // 2 + off) % 4)
            g = dot_nn(local_cols(c), ohl[chunk]).astype(BF16)
            for p in range(2):
                ls[k, chunk * 2 + p] = g[:, p * HALF : (p + 1) * HALF]
            for p in range(2):
                send_first(k, chunk * 2 + p)
            return 0

        lax.fori_loop(0, 8 if only is None else 4, body, 0)

    def layout_turn(k):
        wait_on(lr.at[k], rsem.at[LAY1 + k])

        def body(i, _):
            chunk = (w // 2 + far_first(i)) % 4
            x = jnp.concatenate(
                [jnp.concatenate([lr[k, g * 8 + j] for j in range(8)], axis=1) for g in range(2)],
                axis=0,
            )
            t = dot_nn(x, perml[chunk]).astype(BF16)
            for p in range(2):
                for g in range(2):
                    ls2[k, chunk * 2 + p, g] = t[g * CH : (g + 1) * CH, p * HALF : (p + 1) * HALF]
            for p in range(2):
                send_second(k, chunk * 2 + p)
            return 0

        lax.fori_loop(0, 4, body, 0)

    def product(c, t, s):
        x = jnp.concatenate([c[2 * s], c[2 * s + 1]], axis=1)
        prods[t] = dot_nt(x, tbuf[t])

    def combine_local(k):
        def body(i, _):
            for j in range(4):
                product(layers[k], i * 4 + j, i * 4 + j)
            return 0

        lax.fori_loop(0, 2, body, 0)

    def mask(t, b):
        return jnp.where(tdst[0, t] == b, 1.0, 0.0).astype(F32)

    def combine_rest(k):
        wait_on(layers[k].at[pl.ds(16, NZ)], rsem.at[HALO2 + k])

        def body(i, _):
            for j in range(4):
                product(layers[k], i * 4 + j, tsrc[0, i * 4 + j])
            return 0

        lax.fori_loop(2, 5, body, 0)
        nxt = layers[k + 1]

        def total(b, _):
            acc = prods[b]
            for t in range(8, NT):
                acc += mask(t, b) * prods[t]
            hop = (acc * invd[b][0:1, :]).astype(BF16)
            nxt[2 * b] = hop[:, :HALF]
            nxt[2 * b + 1] = hop[:, HALF:]
            return 0

        lax.fori_loop(0, 8, total, 0)

    def build_ph(i, _):
        m = lax.broadcasted_iota(I32, (1, 256), 1) + i * 256
        build(permh, i, ((m >> 3) & 15) * 64 + (m >> 7) * 8 + (m & 7), 1024)
        return 0

    lax.fori_loop(0, 4, build_ph, 0)

    row16 = lax.broadcasted_iota(I32, (16, 1024), 0)
    h = permute(halves(hidx[...], 0, 1, row16).astype(BF16), permh)
    hp = (h[0:1] * 8.0 + h[1:2]).astype(I32)
    for i in range(4):
        hix[i : i + 1, :] = hp[:, i * 256 : (i + 1) * 256]

    def build_h(i, _):
        build(ohh, i, hix[pl.ds(i, 1), :], 2048)
        return 0

    lax.fori_loop(0, 4, build_h, 0)

    def build_pl(i, _):
        m = lax.broadcasted_iota(I32, (1, 256), 1) + i * 256
        build(perml, i, ((m >> 4) & 7) * 128 + (m >> 7) * 16 + (m & 15), 1024)
        return 0

    lax.fori_loop(0, 4, build_pl, 0)
    order = oidx[...]
    for m in range(16):
        if m < 8:
            picks = [j * 256 + m * 32 for j in range(8)]
        else:
            picks = [(m - 8) * 256 + j * 32 + 16 for j in range(8)]
        oix[m // 2 : m // 2 + 1, m % 2 * HALF : (m % 2 + 1) * HALF] = regroup(order, picks, 16)

    wait_on(c0.at[pl.ds(0, 16)], rsem.at[REP])
    halo_start(0)

    def build_l(i, _):
        build(ohl, i, oix[pl.ds(i, 1), :], 2048)
        return 0

    lax.fori_loop(0, 8, build_l, 0)
    layout_start(0, "z")
    halo_turn(0)
    layout_start(0, "y")
    load_t.wait()

    def row_sums(i, _):
        for j in range(4):
            prods[i * 4 + j, 0:16, :] = dot_nt(jnp.ones((16, 256), BF16), tbuf[i * 4 + j])
        return 0

    lax.fori_loop(0, 5, row_sums, 0)

    def degrees(b, _):
        acc = prods[b, 0:8, :]
        for t in range(8, NT):
            acc += mask(t, b) * prods[t, 0:8, :]
        invd[b] = 1.0 / acc
        return 0

    lax.fori_loop(0, 8, degrees, 0)
    combine_local(0)

    nat = pidx[...]
    for m in range(16):
        own = nat[:, m * HALF : (m + 1) * HALF]
        picks = [(m % 2 * 4 + j) * 256 + m // 2 * 32 for j in range(4)]
        turned = regroup(nat, picks, 32)
        pix[m // 2 : m // 2 + 1, m % 2 * HALF : (m % 2 + 1) * HALF] = jnp.where(core == 0, own, turned)

    def build_p(i, _):
        build(ohp, i, pix[pl.ds(i, 1), :], 2048)
        return 0

    lax.fori_loop(0, 8, build_p, 0)
    combine_rest(0)
    halo_start(1)
    layout_turn(0)
    layout_start(1)
    halo_turn(1)
    combine_local(1)
    layout_turn(1)
    combine_rest(1)
    layout_start(2)

    def arrived(k, m):
        return jnp.concatenate([arr[k, m, 0], arr[k, m, 1]], axis=1)

    for k in range(2):
        wait_on(arr.at[k], rsem.at[LAY2 + k])

    def place(j, _):
        rows = pl.ds(pl.multiple_of(j * 256, 256), 256)
        acc = jnp.zeros((2 * CH, 256), F32)
        for m in range(NZ):
            x = jnp.concatenate([arrived(0, m), arrived(1, m)], axis=0)
            acc += dot_nt(x, ohp[m, rows, :])
        res = acc.astype(BF16)
        for k in range(2):
            out[k, :, rows] = res[k * CH : (k + 1) * CH]
        return 0

    lax.fori_loop(0, 4, place, 0)
    layout_turn(2)
    lax.fori_loop(4, 8, place, 0)
    total2[...] = jnp.zeros((CH, 2048), F32)

    def place_last(i, _):
        step = (i + 1) // 2
        m = (w + jnp.where(i % 2 == 0, step, NZ - step)) % NZ
        wait_on(arr.at[2, m], rsem.at[LAST + m])
        total2[...] += dot_nt(arrived(2, m), ohp[m])
        return 0

    lax.fori_loop(0, NZ, place_last, 0)
    out[2] = total2[...].astype(BF16)

    wait_on(rs.at[pl.ds(0, NREP - 1)], ssem.at[REP])
    for k in range(2):
        wait_on(hs.at[k, pl.ds(0, NA - 1)], ssem.at[HALO1 + k])
        wait_on(ts.at[k, pl.ds(0, NZ - 1)], ssem.at[HALO2 + k])
    for k in range(3):
        wait_on(ls.at[k, pl.ds(0, NA - 1)], ssem.at[LAY1 + k])
        wait_on(ls2.at[k, pl.ds(0, NZ - 1)], ssem.at[LAY2 + k])


def on_device(features, sketch_matrix, tiles, tile_dst, tile_src, halo_index, send_order, arrival_place):
    vm, sm, hbm = (pl.BlockSpec(memory_space=s) for s in (pltpu.VMEM, pltpu.SMEM, pl.ANY))
    return pl.pallas_call(
        kernel,
        out_shape=pltpu.VMEM((3, CH, 2048), BF16),
        in_specs=[hbm, hbm, hbm, sm, sm, vm, vm, vm],
        out_specs=vm,
        scratch_shapes=[
            pltpu.VMEM((512, 768), BF16),
            pltpu.VMEM((768, 256), BF16),
            pltpu.VMEM((NT, 256, 256), BF16),
            pltpu.VMEM((24, CH, HALF), BF16),
            pltpu.VMEM((24, CH, HALF), BF16),
            pltpu.VMEM((16, CH, HALF), BF16),
            pltpu.VMEM((NREP, 4, CH, HALF), BF16),
            pltpu.VMEM((2, NA, 32, HALF), BF16),
            pltpu.VMEM((2, NA, 32, HALF), BF16),
            pltpu.VMEM((CH, 1024), BF16),
            pltpu.VMEM((2, NZ, CH, HALF), BF16),
            pltpu.VMEM((3, NA, CH, HALF), BF16),
            pltpu.VMEM((3, NA, CH, HALF), BF16),
            pltpu.VMEM((3, NZ, 2, CH, HALF), BF16),
            pltpu.VMEM((3, NZ, 2, CH, HALF), BF16),
            pltpu.VMEM((4, 2048, 256), BF16),
            pltpu.VMEM((8, 2048, 256), BF16),
            pltpu.VMEM((8, 2048, 256), BF16),
            pltpu.VMEM((4, 1024, 256), BF16),
            pltpu.VMEM((4, 1024, 256), BF16),
            pltpu.VMEM((4, 256), I32),
            pltpu.VMEM((8, 256), I32),
            pltpu.VMEM((8, 256), I32),
            pltpu.VMEM((NT, CH, 256), F32),
            pltpu.VMEM((CH, 2048), F32),
            pltpu.VMEM((8, 8, 256), F32),
            pltpu.SemaphoreType.DMA((3,)),
            pltpu.SemaphoreType.DMA((11,)),
            pltpu.SemaphoreType.DMA((19,)),
        ],
        compiler_params=pltpu.CompilerParams(
            collective_id=0, has_side_effects=True, vmem_limit_bytes=56 * 2**20
        ),
    )(features, sketch_matrix, tiles[0], tile_dst, tile_src, halo_index, send_order, arrival_place)


def solution(mesh):
    in_specs = (
        P(("dom", "rep"), None),
        P(),
        P("dom", None, None, None),
        P("dom", None),
        P("dom", None),
        P("dom", None),
        P("dom", None),
        P("dom", None),
    )
    return jax.shard_map(
        on_device, mesh=mesh, in_specs=in_specs, out_specs=P(None, "rep", "dom"), check_vma=False
    )
```

```python
import jax
import jax.numpy as jnp
from jax import lax
from jax.experimental import pallas as pl
from jax.experimental.pallas import tpu as pltpu
from jax.sharding import PartitionSpec as P

MESH = pl.DeviceIdType.MESH
BF16, F32, I32 = jnp.bfloat16, jnp.float32, jnp.int32
NZ = 8
NA = 16
NREP = 4
CH = 64
NT = 20
HALF = 128

REP, HALO1, HALO2, LAY1, LAY2, LAST = 0, 1, 3, 5, 8, 11


def dot_nt(a, b):
    return lax.dot_general(a, b, (((1,), (1,)), ((), ())), preferred_element_type=F32)


def dot_nn(a, b):
    return lax.dot_general(a, b, (((1,), (0,)), ((), ())), preferred_element_type=F32)


def build(ref, chunk, idx, rows):
    step = 64
    width = idx.shape[1]

    def body(r, _):
        base = pl.multiple_of(r * step, step)
        row = lax.broadcasted_iota(I32, (step, width), 0)
        hot = jnp.where(row == idx - base, 1.0, 0.0).astype(BF16)
        ref[chunk, pl.ds(base, step), :] = hot
        return 0

    lax.fori_loop(0, rows // step, body, 0)


def far_first(i):
    return jnp.where(i == 0, 2, jnp.where(i == 1, 1, jnp.where(i == 2, 3, 0)))


def regroup(row, picks, width):
    lane = lax.broadcasted_iota(I32, (1, HALF), 1)
    out = jnp.zeros((1, HALF), I32)
    for j, start in enumerate(picks):
        base = start // HALF * HALF
        piece = pltpu.roll(row[:, base : base + HALF], (j * width - (start - base)) % HALF, 1)
        out = jnp.where(lane // width == j, piece, out)
    return out


def permute(x, perm):
    return sum(dot_nt(x[:, c * 256 : (c + 1) * 256], perm[c]) for c in range(4))


def halves(idx, first, second, row):
    hi, lo = (idx >> 3).astype(F32), (idx & 7).astype(F32)
    return jnp.where(row == first, hi, jnp.where(row == second, lo, 0.0))


def kernel(
    feat, sketch, tiles, tdst, tsrc, hidx, oidx, pidx, out,
    fbuf, sbuf, tbuf, c0, c1, c2, rs, hs, hr, ub, ts, ls, lr, ls2, arr,
    ohh, ohl, ohp, permh, perml, hix, oix, pix, prods, total2, invd, lsem, ssem, rsem,
):
    dom = lax.axis_index("dom")
    rep = lax.axis_index("rep")
    z = dom // NA
    a = dom % NA
    y = a // 2
    core = a % 2
    w = jnp.where(core == 0, z, y)
    layers = (c0, c1, c2)

    load_f = [
        pltpu.make_async_copy(feat.at[rows], fbuf.at[rows], lsem.at[sem])
        for rows, sem in ((pl.ds(0, 256), 0), (pl.ds(256, 256), 3))
    ]
    load_s = pltpu.make_async_copy(sketch, sbuf, lsem.at[1])
    load_t = pltpu.make_async_copy(tiles, tbuf, lsem.at[2])
    load_s.start()
    for half in load_f:
        half.start()

    barrier = pltpu.get_barrier_semaphore()

    def greet(o, _):
        pl.semaphore_signal(
            barrier, inc=1, device_id=(z * NA + (a + o) % NA, rep), device_id_type=MESH
        )
        return 0

    def greet_z(o, _):
        for i in range(2):
            pl.semaphore_signal(
                barrier, inc=1, device_id=((z + o) % NZ * NA + y * 2 + i, rep), device_id_type=MESH
            )
        return 0

    def greet_rep(o, _):
        pl.semaphore_signal(
            barrier, inc=1, device_id=(dom, (rep + o) % NREP), device_id_type=MESH
        )
        return 0

    lax.fori_loop(1, NREP, greet_rep, 0)
    lax.fori_loop(1, NA, greet, 0)
    lax.fori_loop(1, NZ, greet_z, 0)

    load_s.wait()
    st = sbuf[...].T
    for h in range(2):
        load_f[h].wait()
        hop = dot_nt(st, fbuf[h * 256 : (h + 1) * 256, :]).astype(BF16)
        for r in range(NREP):
            for k in range(2):
                rs[r, 2 * h + k] = hop[r * CH : (r + 1) * CH, k * HALF : (k + 1) * HALF]

    load_t.start()
    pl.semaphore_wait(barrier, NREP - 1 + NA - 1 + 2 * (NZ - 1))

    mine = c0.at[pl.ds(rep * 4, 4)]

    def send_rep(o, _):
        to = (rep + jnp.where(o == 1, 2, jnp.where(o == 2, 1, 3))) % NREP
        pltpu.make_async_remote_copy(
            src_ref=rs.at[to], dst_ref=mine, send_sem=ssem.at[REP], recv_sem=rsem.at[REP],
            device_id=(dom, to), device_id_type=MESH,
        ).start()
        return 0

    lax.fori_loop(1, NREP, send_rep, 0)
    pltpu.make_async_copy(rs.at[rep], mine, rsem.at[REP]).start()

    def wait_on(ref, sem):
        pltpu.make_async_copy(ref, ref, sem).wait()

    def send_a(src, dst, row, to):
        @pl.when(to != a)
        def _():
            pltpu.make_async_remote_copy(
                src_ref=src.at[to], dst_ref=dst.at[a], send_sem=ssem.at[row],
                recv_sem=rsem.at[row], device_id=(z * NA + to, rep), device_id_type=MESH,
            ).start()

        @pl.when(to == a)
        def _():
            pltpu.make_async_copy(src.at[to], dst.at[a], rsem.at[row]).start()

    def send_z(src, dst, row, to):
        @pl.when(to != z)
        def _():
            pltpu.make_async_remote_copy(
                src_ref=src.at[to], dst_ref=dst.at[z], send_sem=ssem.at[row],
                recv_sem=rsem.at[row], device_id=(to * NA + a, rep), device_id_type=MESH,
            ).start()

        @pl.when(to == z)
        def _():
            pltpu.make_async_copy(src.at[to], dst.at[z], rsem.at[row]).start()

    def send_first(k, m):
        to = jnp.where(m < 8, z * NA + m * 2, (m - 8) * NA + y * 2 + 1)
        slot = jnp.where(m < 8, a, z * 2 + core)
        row = LAY1 + k

        @pl.when(to != dom)
        def _():
            pltpu.make_async_remote_copy(
                src_ref=ls.at[k, m], dst_ref=lr.at[k, slot], send_sem=ssem.at[row],
                recv_sem=rsem.at[row], device_id=(to, rep), device_id_type=MESH,
            ).start()

        @pl.when(to == dom)
        def _():
            pltpu.make_async_copy(ls.at[k, m], lr.at[k, slot], rsem.at[row]).start()

    def send_second(k, m):
        to = jnp.where(core == 0, m * NA + a, z * NA + m * 2 + 1)
        got = rsem.at[LAST + w] if k == 2 else rsem.at[LAY2 + k]

        @pl.when(m != w)
        def _():
            pltpu.make_async_remote_copy(
                src_ref=ls2.at[k, m], dst_ref=arr.at[k, w], send_sem=ssem.at[LAY2 + k],
                recv_sem=got, device_id=(to, rep), device_id_type=MESH,
            ).start()

        @pl.when(m == w)
        def _():
            pltpu.make_async_copy(ls2.at[k, m], arr.at[k, w], got).start()

    def local_cols(c):
        return jnp.concatenate([c[i] for i in range(16)], axis=1)

    low = lax.broadcasted_iota(I32, (32, HALF), 1) < CH

    def halo_start(k):
        c = layers[k]

        def body(i, _):
            chunk = (a // 4 + far_first(i)) % 4
            g = dot_nn(local_cols(c), ohh[chunk])
            for p in range(2):
                top = g[0:32, p * HALF : (p + 1) * HALF]
                bot = g[32:64, p * HALF : (p + 1) * HALF]
                hs[k, chunk * 4 + 2 * p] = jnp.where(low, top, pltpu.roll(bot, CH, 1)).astype(BF16)
                hs[k, chunk * 4 + 2 * p + 1] = jnp.where(low, pltpu.roll(top, CH, 1), bot).astype(BF16)
            for j in range(4):
                send_a(hs.at[k], hr.at[k], HALO1 + k, chunk * 4 + j)
            return 0

        lax.fori_loop(0, 4, body, 0)

    def halo_turn(k):
        wait_on(hr.at[k], rsem.at[HALO1 + k])
        for q in range(8):
            r0 = hr[k, 2 * q].astype(F32)
            r1 = hr[k, 2 * q + 1].astype(F32)
            ub[0:32, q * HALF : (q + 1) * HALF] = jnp.where(low, r0, pltpu.roll(r1, CH, 1)).astype(BF16)
            ub[32:64, q * HALF : (q + 1) * HALF] = jnp.where(low, pltpu.roll(r0, CH, 1), r1).astype(BF16)
        dst = layers[k].at[pl.ds(16, NZ)]

        def body(i, _):
            chunk = (z // 2 + far_first(i)) % 4
            t = dot_nn(ub[...], permh[chunk]).astype(BF16)
            for p in range(2):
                ts[k, chunk * 2 + p] = t[:, p * HALF : (p + 1) * HALF]
            for p in range(2):
                send_z(ts.at[k], dst, HALO2 + k, chunk * 2 + p)
            return 0

        lax.fori_loop(0, 4, body, 0)

    def layout_start(k, only=None):
        c = layers[k]

        def body(i, _):
            off = far_first(i // 2 if only is None else i)
            over_y = i % 2 == 0 if only is None else only == "y"
            chunk = jnp.where(over_y, (y // 2 + off) % 4, 4 + (z // 2 + off) % 4)
            g = dot_nn(local_cols(c), ohl[chunk]).astype(BF16)
            for p in range(2):
                ls[k, chunk * 2 + p] = g[:, p * HALF : (p + 1) * HALF]
            for p in range(2):
                send_first(k, chunk * 2 + p)
            return 0

        lax.fori_loop(0, 8 if only is None else 4, body, 0)

    def layout_turn(k):
        wait_on(lr.at[k], rsem.at[LAY1 + k])

        def body(i, _):
            chunk = (w // 2 + far_first(i)) % 4
            x = jnp.concatenate(
                [jnp.concatenate([lr[k, g * 8 + j] for j in range(8)], axis=1) for g in range(2)],
                axis=0,
            )
            t = dot_nn(x, perml[chunk]).astype(BF16)
            for p in range(2):
                for g in range(2):
                    ls2[k, chunk * 2 + p, g] = t[g * CH : (g + 1) * CH, p * HALF : (p + 1) * HALF]
            for p in range(2):
                send_second(k, chunk * 2 + p)
            return 0

        lax.fori_loop(0, 4, body, 0)

    def product(c, t, s):
        x = jnp.concatenate([c[2 * s], c[2 * s + 1]], axis=1)
        prods[t] = dot_nt(x, tbuf[t])

    def combine_local(k):
        def body(i, _):
            for j in range(4):
                product(layers[k], i * 4 + j, i * 4 + j)
            return 0

        lax.fori_loop(0, 2, body, 0)

    def mask(t, b):
        return jnp.where(tdst[0, t] == b, 1.0, 0.0).astype(F32)

    def combine_rest(k):
        wait_on(layers[k].at[pl.ds(16, NZ)], rsem.at[HALO2 + k])

        def body(i, _):
            for j in range(4):
                product(layers[k], i * 4 + j, tsrc[0, i * 4 + j])
            return 0

        lax.fori_loop(2, 5, body, 0)
        nxt = layers[k + 1]

        def total(b, _):
            acc = prods[b]
            for t in range(8, NT):
                acc += mask(t, b) * prods[t]
            hop = (acc * invd[b][0:1, :]).astype(BF16)
            nxt[2 * b] = hop[:, :HALF]
            nxt[2 * b + 1] = hop[:, HALF:]
            return 0

        lax.fori_loop(0, 8, total, 0)

    def build_ph(i, _):
        m = lax.broadcasted_iota(I32, (1, 256), 1) + i * 256
        build(permh, i, ((m >> 3) & 15) * 64 + (m >> 7) * 8 + (m & 7), 1024)
        return 0

    lax.fori_loop(0, 4, build_ph, 0)

    row16 = lax.broadcasted_iota(I32, (16, 1024), 0)
    h = permute(halves(hidx[...], 0, 1, row16).astype(BF16), permh)
    hp = (h[0:1] * 8.0 + h[1:2]).astype(I32)
    for i in range(4):
        hix[i : i + 1, :] = hp[:, i * 256 : (i + 1) * 256]

    def build_h(i, _):
        build(ohh, i, hix[pl.ds(i, 1), :], 2048)
        return 0

    lax.fori_loop(0, 4, build_h, 0)

    def build_pl(i, _):
        m = lax.broadcasted_iota(I32, (1, 256), 1) + i * 256
        build(perml, i, ((m >> 4) & 7) * 128 + (m >> 7) * 16 + (m & 15), 1024)
        return 0

    lax.fori_loop(0, 4, build_pl, 0)
    order = oidx[...]
    for m in range(16):
        if m < 8:
            picks = [j * 256 + m * 32 for j in range(8)]
        else:
            picks = [(m - 8) * 256 + j * 32 + 16 for j in range(8)]
        oix[m // 2 : m // 2 + 1, m % 2 * HALF : (m % 2 + 1) * HALF] = regroup(order, picks, 16)

    wait_on(c0.at[pl.ds(0, 16)], rsem.at[REP])
    halo_start(0)

    def build_l(i, _):
        build(ohl, i, oix[pl.ds(i, 1), :], 2048)
        return 0

    lax.fori_loop(0, 8, build_l, 0)
    layout_start(0, "z")
    halo_turn(0)
    layout_start(0, "y")
    load_t.wait()

    def row_sums(i, _):
        for j in range(4):
            prods[i * 4 + j, 0:16, :] = dot_nt(jnp.ones((16, 256), BF16), tbuf[i * 4 + j])
        return 0

    lax.fori_loop(0, 5, row_sums, 0)

    def degrees(b, _):
        acc = prods[b, 0:8, :]
        for t in range(8, NT):
            acc += mask(t, b) * prods[t, 0:8, :]
        invd[b] = 1.0 / acc
        return 0

    lax.fori_loop(0, 8, degrees, 0)
    combine_local(0)

    nat = pidx[...]
    for m in range(16):
        own = nat[:, m * HALF : (m + 1) * HALF]
        picks = [(m % 2 * 4 + j) * 256 + m // 2 * 32 for j in range(4)]
        turned = regroup(nat, picks, 32)
        pix[m // 2 : m // 2 + 1, m % 2 * HALF : (m % 2 + 1) * HALF] = jnp.where(core == 0, own, turned)

    def build_p(i, _):
        build(ohp, i, pix[pl.ds(i, 1), :], 2048)
        return 0

    lax.fori_loop(0, 8, build_p, 0)
    combine_rest(0)
    halo_start(1)
    layout_turn(0)
    layout_start(1)
    halo_turn(1)
    combine_local(1)
    layout_turn(1)
    combine_rest(1)
    layout_start(2)

    def arrived(k, m):
        return jnp.concatenate([arr[k, m, 0], arr[k, m, 1]], axis=1)

    for k in range(2):
        wait_on(arr.at[k], rsem.at[LAY2 + k])

    def place(j, _):
        rows = pl.ds(pl.multiple_of(j * 256, 256), 256)
        acc = jnp.zeros((2 * CH, 256), F32)
        for m in range(NZ):
            x = jnp.concatenate([arrived(0, m), arrived(1, m)], axis=0)
            acc += dot_nt(x, ohp[m, rows, :])
        res = acc.astype(BF16)
        for k in range(2):
            out[k, :, rows] = res[k * CH : (k + 1) * CH]
        return 0

    lax.fori_loop(0, 4, place, 0)
    layout_turn(2)
    lax.fori_loop(4, 8, place, 0)
    total2[...] = jnp.zeros((CH, 2048), F32)

    def place_last(i, _):
        step = (i + 1) // 2
        m = (w + jnp.where(i % 2 == 0, step, NZ - step)) % NZ
        wait_on(arr.at[2, m], rsem.at[LAST + m])
        total2[...] += dot_nt(arrived(2, m), ohp[m])
        return 0

    lax.fori_loop(0, NZ, place_last, 0)
    out[2] = total2[...].astype(BF16)

    wait_on(rs.at[pl.ds(0, NREP - 1)], ssem.at[REP])
    for k in range(2):
        wait_on(hs.at[k, pl.ds(0, NA - 1)], ssem.at[HALO1 + k])
        wait_on(ts.at[k, pl.ds(0, NZ - 1)], ssem.at[HALO2 + k])
    for k in range(3):
        wait_on(ls.at[k, pl.ds(0, NA - 1)], ssem.at[LAY1 + k])
        wait_on(ls2.at[k, pl.ds(0, NZ - 1)], ssem.at[LAY2 + k])


def on_device(features, sketch_matrix, tiles, tile_dst, tile_src, halo_index, send_order, arrival_place):
    vm, sm, hbm = (pl.BlockSpec(memory_space=s) for s in (pltpu.VMEM, pltpu.SMEM, pl.ANY))
    return pl.pallas_call(
        kernel,
        out_shape=pltpu.VMEM((3, CH, 2048), BF16),
        in_specs=[hbm, hbm, hbm, sm, sm, vm, vm, vm],
        out_specs=vm,
        scratch_shapes=[
            pltpu.VMEM((512, 768), BF16),
            pltpu.VMEM((768, 256), BF16),
            pltpu.VMEM((NT, 256, 256), BF16),
            pltpu.VMEM((24, CH, HALF), BF16),
            pltpu.VMEM((24, CH, HALF), BF16),
            pltpu.VMEM((16, CH, HALF), BF16),
            pltpu.VMEM((NREP, 4, CH, HALF), BF16),
            pltpu.VMEM((2, NA, 32, HALF), BF16),
            pltpu.VMEM((2, NA, 32, HALF), BF16),
            pltpu.VMEM((CH, 1024), BF16),
            pltpu.VMEM((2, NZ, CH, HALF), BF16),
            pltpu.VMEM((3, NA, CH, HALF), BF16),
            pltpu.VMEM((3, NA, CH, HALF), BF16),
            pltpu.VMEM((3, NZ, 2, CH, HALF), BF16),
            pltpu.VMEM((3, NZ, 2, CH, HALF), BF16),
            pltpu.VMEM((4, 2048, 256), BF16),
            pltpu.VMEM((8, 2048, 256), BF16),
            pltpu.VMEM((8, 2048, 256), BF16),
            pltpu.VMEM((4, 1024, 256), BF16),
            pltpu.VMEM((4, 1024, 256), BF16),
            pltpu.VMEM((4, 256), I32),
            pltpu.VMEM((8, 256), I32),
            pltpu.VMEM((8, 256), I32),
            pltpu.VMEM((NT, CH, 256), F32),
            pltpu.VMEM((CH, 2048), F32),
            pltpu.VMEM((8, 8, 256), F32),
            pltpu.SemaphoreType.DMA((4,)),
            pltpu.SemaphoreType.DMA((11,)),
            pltpu.SemaphoreType.DMA((19,)),
        ],
        compiler_params=pltpu.CompilerParams(
            collective_id=0, has_side_effects=True, vmem_limit_bytes=56 * 2**20
        ),
    )(features, sketch_matrix, tiles[0], tile_dst, tile_src, halo_index, send_order, arrival_place)


def solution(mesh):
    in_specs = (
        P(("dom", "rep"), None),
        P(),
        P("dom", None, None, None),
        P("dom", None),
        P("dom", None),
        P("dom", None),
        P("dom", None),
        P("dom", None),
    )
    return jax.shard_map(
        on_device, mesh=mesh, in_specs=in_specs, out_specs=P(None, "rep", "dom"), check_vma=False
    )
```

```python
import jax
import jax.numpy as jnp
from jax import lax
from jax.experimental import pallas as pl
from jax.experimental.pallas import tpu as pltpu
from jax.sharding import PartitionSpec as P

MESH = pl.DeviceIdType.MESH
BF16, F32, I32 = jnp.bfloat16, jnp.float32, jnp.int32
NZ = 8
NA = 16
NREP = 4
CH = 64
NT = 20
HALF = 128

REP, HALO1, HALO2, LAY1, LAY2, LAST = 0, 1, 3, 5, 8, 11


def dot_nt(a, b):
    return lax.dot_general(a, b, (((1,), (1,)), ((), ())), preferred_element_type=F32)


def dot_nn(a, b):
    return lax.dot_general(a, b, (((1,), (0,)), ((), ())), preferred_element_type=F32)


def build(ref, chunk, idx, rows):
    step = 64
    width = idx.shape[1]

    def body(r, _):
        base = pl.multiple_of(r * step, step)
        row = lax.broadcasted_iota(I32, (step, width), 0)
        hot = jnp.where(row == idx - base, 1.0, 0.0).astype(BF16)
        ref[chunk, pl.ds(base, step), :] = hot
        return 0

    lax.fori_loop(0, rows // step, body, 0)


def far_first(i):
    return jnp.where(i == 0, 2, jnp.where(i == 1, 1, jnp.where(i == 2, 3, 0)))


def regroup(row, picks, width):
    lane = lax.broadcasted_iota(I32, (1, HALF), 1)
    out = jnp.zeros((1, HALF), I32)
    for j, start in enumerate(picks):
        base = start // HALF * HALF
        piece = pltpu.roll(row[:, base : base + HALF], (j * width - (start - base)) % HALF, 1)
        out = jnp.where(lane // width == j, piece, out)
    return out


def permute(x, perm):
    return sum(dot_nt(x[:, c * 256 : (c + 1) * 256], perm[c]) for c in range(4))


def halves(idx, first, second, row):
    hi, lo = (idx >> 3).astype(F32), (idx & 7).astype(F32)
    return jnp.where(row == first, hi, jnp.where(row == second, lo, 0.0))


def kernel(
    feat, sketch, tiles, tdst, tsrc, hidx, oidx, pidx, out,
    fbuf, sbuf, tbuf, c0, c1, c2, rs, hs, hr, ub, ts, ls, lr, ls2, arr,
    ohh, ohl, ohp, permh, perml, hix, oix, pix, prods, total2, invd, lsem, ssem, rsem,
):
    dom = lax.axis_index("dom")
    rep = lax.axis_index("rep")
    z = dom // NA
    a = dom % NA
    y = a // 2
    core = a % 2
    w = jnp.where(core == 0, z, y)
    layers = (c0, c1, c2)

    load_f = pltpu.make_async_copy(feat, fbuf, lsem.at[0])
    load_s = pltpu.make_async_copy(sketch, sbuf, lsem.at[1])
    load_t = pltpu.make_async_copy(tiles, tbuf, lsem.at[2])
    load_s.start()
    load_f.start()
    load_t.start()

    barrier = pltpu.get_barrier_semaphore()

    def greet(o, _):
        pl.semaphore_signal(
            barrier, inc=1, device_id=(z * NA + (a + o) % NA, rep), device_id_type=MESH
        )
        return 0

    def greet_z(o, _):
        for i in range(2):
            pl.semaphore_signal(
                barrier, inc=1, device_id=((z + o) % NZ * NA + y * 2 + i, rep), device_id_type=MESH
            )
        return 0

    def greet_rep(o, _):
        pl.semaphore_signal(
            barrier, inc=1, device_id=(dom, (rep + o) % NREP), device_id_type=MESH
        )
        return 0

    lax.fori_loop(1, NREP, greet_rep, 0)
    lax.fori_loop(1, NA, greet, 0)
    lax.fori_loop(1, NZ, greet_z, 0)

    load_s.wait()
    st = sbuf[...].T
    load_f.wait()
    for h in range(2):
        hop = dot_nt(st, fbuf[h * 256 : (h + 1) * 256, :]).astype(BF16)
        for r in range(NREP):
            for k in range(2):
                rs[r, 2 * h + k] = hop[r * CH : (r + 1) * CH, k * HALF : (k + 1) * HALF]

    pl.semaphore_wait(barrier, NREP - 1 + NA - 1 + 2 * (NZ - 1))

    mine = c0.at[pl.ds(rep * 4, 4)]

    def send_rep(o, _):
        to = (rep + jnp.where(o == 1, 2, jnp.where(o == 2, 1, 3))) % NREP
        pltpu.make_async_remote_copy(
            src_ref=rs.at[to], dst_ref=mine, send_sem=ssem.at[REP], recv_sem=rsem.at[REP],
            device_id=(dom, to), device_id_type=MESH,
        ).start()
        return 0

    lax.fori_loop(1, NREP, send_rep, 0)
    pltpu.make_async_copy(rs.at[rep], mine, rsem.at[REP]).start()

    def wait_on(ref, sem):
        pltpu.make_async_copy(ref, ref, sem).wait()

    def send_a(src, dst, row, to):
        @pl.when(to != a)
        def _():
            pltpu.make_async_remote_copy(
                src_ref=src.at[to], dst_ref=dst.at[a], send_sem=ssem.at[row],
                recv_sem=rsem.at[row], device_id=(z * NA + to, rep), device_id_type=MESH,
            ).start()

        @pl.when(to == a)
        def _():
            pltpu.make_async_copy(src.at[to], dst.at[a], rsem.at[row]).start()

    def send_z(src, dst, row, to):
        @pl.when(to != z)
        def _():
            pltpu.make_async_remote_copy(
                src_ref=src.at[to], dst_ref=dst.at[z], send_sem=ssem.at[row],
                recv_sem=rsem.at[row], device_id=(to * NA + a, rep), device_id_type=MESH,
            ).start()

        @pl.when(to == z)
        def _():
            pltpu.make_async_copy(src.at[to], dst.at[z], rsem.at[row]).start()

    def send_first(k, m):
        to = jnp.where(m < 8, z * NA + m * 2, (m - 8) * NA + y * 2 + 1)
        slot = jnp.where(m < 8, a, z * 2 + core)
        row = LAY1 + k

        @pl.when(to != dom)
        def _():
            pltpu.make_async_remote_copy(
                src_ref=ls.at[k, m], dst_ref=lr.at[k, slot], send_sem=ssem.at[row],
                recv_sem=rsem.at[row], device_id=(to, rep), device_id_type=MESH,
            ).start()

        @pl.when(to == dom)
        def _():
            pltpu.make_async_copy(ls.at[k, m], lr.at[k, slot], rsem.at[row]).start()

    def send_second(k, m):
        to = jnp.where(core == 0, m * NA + a, z * NA + m * 2 + 1)
        got = rsem.at[LAST + w] if k == 2 else rsem.at[LAY2 + k]

        @pl.when(m != w)
        def _():
            pltpu.make_async_remote_copy(
                src_ref=ls2.at[k, m], dst_ref=arr.at[k, w], send_sem=ssem.at[LAY2 + k],
                recv_sem=got, device_id=(to, rep), device_id_type=MESH,
            ).start()

        @pl.when(m == w)
        def _():
            pltpu.make_async_copy(ls2.at[k, m], arr.at[k, w], got).start()

    def local_cols(c):
        return jnp.concatenate([c[i] for i in range(16)], axis=1)

    low = lax.broadcasted_iota(I32, (32, HALF), 1) < CH

    def halo_start(k):
        c = layers[k]

        def body(i, _):
            chunk = (a // 4 + far_first(i)) % 4
            g = dot_nn(local_cols(c), ohh[chunk])
            for p in range(2):
                top = g[0:32, p * HALF : (p + 1) * HALF]
                bot = g[32:64, p * HALF : (p + 1) * HALF]
                hs[k, chunk * 4 + 2 * p] = jnp.where(low, top, pltpu.roll(bot, CH, 1)).astype(BF16)
                hs[k, chunk * 4 + 2 * p + 1] = jnp.where(low, pltpu.roll(top, CH, 1), bot).astype(BF16)
            for j in range(4):
                send_a(hs.at[k], hr.at[k], HALO1 + k, chunk * 4 + j)
            return 0

        lax.fori_loop(0, 4, body, 0)

    def halo_turn(k):
        wait_on(hr.at[k], rsem.at[HALO1 + k])
        for q in range(8):
            r0 = hr[k, 2 * q].astype(F32)
            r1 = hr[k, 2 * q + 1].astype(F32)
            ub[0:32, q * HALF : (q + 1) * HALF] = jnp.where(low, r0, pltpu.roll(r1, CH, 1)).astype(BF16)
            ub[32:64, q * HALF : (q + 1) * HALF] = jnp.where(low, pltpu.roll(r0, CH, 1), r1).astype(BF16)
        dst = layers[k].at[pl.ds(16, NZ)]

        def body(i, _):
            chunk = (z // 2 + far_first(i)) % 4
            t = dot_nn(ub[...], permh[chunk]).astype(BF16)
            for p in range(2):
                ts[k, chunk * 2 + p] = t[:, p * HALF : (p + 1) * HALF]
            for p in range(2):
                send_z(ts.at[k], dst, HALO2 + k, chunk * 2 + p)
            return 0

        lax.fori_loop(0, 4, body, 0)

    def layout_start(k, only=None):
        c = layers[k]

        def body(i, _):
            off = far_first(i // 2 if only is None else i)
            over_y = i % 2 == 0 if only is None else only == "y"
            chunk = jnp.where(over_y, (y // 2 + off) % 4, 4 + (z // 2 + off) % 4)
            g = dot_nn(local_cols(c), ohl[chunk]).astype(BF16)
            for p in range(2):
                ls[k, chunk * 2 + p] = g[:, p * HALF : (p + 1) * HALF]
            for p in range(2):
                send_first(k, chunk * 2 + p)
            return 0

        lax.fori_loop(0, 8 if only is None else 4, body, 0)

    def layout_turn(k):
        wait_on(lr.at[k], rsem.at[LAY1 + k])

        def body(i, _):
            chunk = (w // 2 + far_first(i)) % 4
            x = jnp.concatenate(
                [jnp.concatenate([lr[k, g * 8 + j] for j in range(8)], axis=1) for g in range(2)],
                axis=0,
            )
            t = dot_nn(x, perml[chunk]).astype(BF16)
            for p in range(2):
                for g in range(2):
                    ls2[k, chunk * 2 + p, g] = t[g * CH : (g + 1) * CH, p * HALF : (p + 1) * HALF]
            for p in range(2):
                send_second(k, chunk * 2 + p)
            return 0

        lax.fori_loop(0, 4, body, 0)

    def product(c, t, s):
        x = jnp.concatenate([c[2 * s], c[2 * s + 1]], axis=1)
        prods[t] = dot_nt(x, tbuf[t])

    def combine_local(k):
        def body(i, _):
            for j in range(4):
                product(layers[k], i * 4 + j, i * 4 + j)
            return 0

        lax.fori_loop(0, 2, body, 0)

    def mask(t, b):
        return jnp.where(tdst[0, t] == b, 1.0, 0.0).astype(F32)

    def combine_rest(k):
        wait_on(layers[k].at[pl.ds(16, NZ)], rsem.at[HALO2 + k])

        def body(i, _):
            for j in range(4):
                product(layers[k], i * 4 + j, tsrc[0, i * 4 + j])
            return 0

        lax.fori_loop(2, 5, body, 0)
        nxt = layers[k + 1]

        def total(b, _):
            acc = prods[b]
            for t in range(8, NT):
                acc += mask(t, b) * prods[t]
            hop = (acc * invd[b][0:1, :]).astype(BF16)
            nxt[2 * b] = hop[:, :HALF]
            nxt[2 * b + 1] = hop[:, HALF:]
            return 0

        lax.fori_loop(0, 8, total, 0)

    def build_ph(i, _):
        m = lax.broadcasted_iota(I32, (1, 256), 1) + i * 256
        build(permh, i, ((m >> 3) & 15) * 64 + (m >> 7) * 8 + (m & 7), 1024)
        return 0

    lax.fori_loop(0, 4, build_ph, 0)

    row16 = lax.broadcasted_iota(I32, (16, 1024), 0)
    h = permute(halves(hidx[...], 0, 1, row16).astype(BF16), permh)
    hp = (h[0:1] * 8.0 + h[1:2]).astype(I32)
    for i in range(4):
        hix[i : i + 1, :] = hp[:, i * 256 : (i + 1) * 256]

    def build_h(i, _):
        build(ohh, i, hix[pl.ds(i, 1), :], 2048)
        return 0

    lax.fori_loop(0, 4, build_h, 0)

    def build_pl(i, _):
        m = lax.broadcasted_iota(I32, (1, 256), 1) + i * 256
        build(perml, i, ((m >> 4) & 7) * 128 + (m >> 7) * 16 + (m & 15), 1024)
        return 0

    lax.fori_loop(0, 4, build_pl, 0)
    order = oidx[...]
    for m in range(16):
        if m < 8:
            picks = [j * 256 + m * 32 for j in range(8)]
        else:
            picks = [(m - 8) * 256 + j * 32 + 16 for j in range(8)]
        oix[m // 2 : m // 2 + 1, m % 2 * HALF : (m % 2 + 1) * HALF] = regroup(order, picks, 16)

    wait_on(c0.at[pl.ds(0, 16)], rsem.at[REP])
    halo_start(0)

    def build_l(i, _):
        build(ohl, i, oix[pl.ds(i, 1), :], 2048)
        return 0

    lax.fori_loop(0, 8, build_l, 0)
    layout_start(0, "z")
    halo_turn(0)
    layout_start(0, "y")
    load_t.wait()

    def row_sums(i, _):
        for j in range(4):
            prods[i * 4 + j, 0:16, :] = dot_nt(jnp.ones((16, 256), BF16), tbuf[i * 4 + j])
        return 0

    lax.fori_loop(0, 5, row_sums, 0)

    def degrees(b, _):
        acc = prods[b, 0:8, :]
        for t in range(8, NT):
            acc += mask(t, b) * prods[t, 0:8, :]
        invd[b] = 1.0 / acc
        return 0

    lax.fori_loop(0, 8, degrees, 0)
    combine_local(0)

    nat = pidx[...]
    for m in range(16):
        own = nat[:, m * HALF : (m + 1) * HALF]
        picks = [(m % 2 * 4 + j) * 256 + m // 2 * 32 for j in range(4)]
        turned = regroup(nat, picks, 32)
        pix[m // 2 : m // 2 + 1, m % 2 * HALF : (m % 2 + 1) * HALF] = jnp.where(core == 0, own, turned)

    def build_p(i, _):
        build(ohp, i, pix[pl.ds(i, 1), :], 2048)
        return 0

    lax.fori_loop(0, 8, build_p, 0)
    combine_rest(0)
    halo_start(1)
    layout_start(1)
    halo_turn(1)
    combine_local(1)
    layout_turn(0)
    layout_turn(1)
    combine_rest(1)
    layout_start(2)

    def arrived(k, m):
        return jnp.concatenate([arr[k, m, 0], arr[k, m, 1]], axis=1)

    for k in range(2):
        wait_on(arr.at[k], rsem.at[LAY2 + k])

    def place(j, _):
        rows = pl.ds(pl.multiple_of(j * 256, 256), 256)
        acc = jnp.zeros((2 * CH, 256), F32)
        for m in range(NZ):
            x = jnp.concatenate([arrived(0, m), arrived(1, m)], axis=0)
            acc += dot_nt(x, ohp[m, rows, :])
        res = acc.astype(BF16)
        for k in range(2):
            out[k, :, rows] = res[k * CH : (k + 1) * CH]
        return 0

    lax.fori_loop(0, 4, place, 0)
    layout_turn(2)
    lax.fori_loop(4, 8, place, 0)
    total2[...] = jnp.zeros((CH, 2048), F32)

    def place_last(i, _):
        step = (i + 1) // 2
        m = (w + jnp.where(i % 2 == 0, step, NZ - step)) % NZ
        wait_on(arr.at[2, m], rsem.at[LAST + m])
        total2[...] += dot_nt(arrived(2, m), ohp[m])
        return 0

    lax.fori_loop(0, NZ, place_last, 0)
    out[2] = total2[...].astype(BF16)

    wait_on(rs.at[pl.ds(0, NREP - 1)], ssem.at[REP])
    for k in range(2):
        wait_on(hs.at[k, pl.ds(0, NA - 1)], ssem.at[HALO1 + k])
        wait_on(ts.at[k, pl.ds(0, NZ - 1)], ssem.at[HALO2 + k])
    for k in range(3):
        wait_on(ls.at[k, pl.ds(0, NA - 1)], ssem.at[LAY1 + k])
        wait_on(ls2.at[k, pl.ds(0, NZ - 1)], ssem.at[LAY2 + k])


def on_device(features, sketch_matrix, tiles, tile_dst, tile_src, halo_index, send_order, arrival_place):
    vm, sm, hbm = (pl.BlockSpec(memory_space=s) for s in (pltpu.VMEM, pltpu.SMEM, pl.ANY))
    return pl.pallas_call(
        kernel,
        out_shape=pltpu.VMEM((3, CH, 2048), BF16),
        in_specs=[hbm, hbm, hbm, sm, sm, vm, vm, vm],
        out_specs=vm,
        scratch_shapes=[
            pltpu.VMEM((512, 768), BF16),
            pltpu.VMEM((768, 256), BF16),
            pltpu.VMEM((NT, 256, 256), BF16),
            pltpu.VMEM((24, CH, HALF), BF16),
            pltpu.VMEM((24, CH, HALF), BF16),
            pltpu.VMEM((16, CH, HALF), BF16),
            pltpu.VMEM((NREP, 4, CH, HALF), BF16),
            pltpu.VMEM((2, NA, 32, HALF), BF16),
            pltpu.VMEM((2, NA, 32, HALF), BF16),
            pltpu.VMEM((CH, 1024), BF16),
            pltpu.VMEM((2, NZ, CH, HALF), BF16),
            pltpu.VMEM((3, NA, CH, HALF), BF16),
            pltpu.VMEM((3, NA, CH, HALF), BF16),
            pltpu.VMEM((3, NZ, 2, CH, HALF), BF16),
            pltpu.VMEM((3, NZ, 2, CH, HALF), BF16),
            pltpu.VMEM((4, 2048, 256), BF16),
            pltpu.VMEM((8, 2048, 256), BF16),
            pltpu.VMEM((8, 2048, 256), BF16),
            pltpu.VMEM((4, 1024, 256), BF16),
            pltpu.VMEM((4, 1024, 256), BF16),
            pltpu.VMEM((4, 256), I32),
            pltpu.VMEM((8, 256), I32),
            pltpu.VMEM((8, 256), I32),
            pltpu.VMEM((NT, CH, 256), F32),
            pltpu.VMEM((CH, 2048), F32),
            pltpu.VMEM((8, 8, 256), F32),
            pltpu.SemaphoreType.DMA((3,)),
            pltpu.SemaphoreType.DMA((11,)),
            pltpu.SemaphoreType.DMA((19,)),
        ],
        compiler_params=pltpu.CompilerParams(
            collective_id=0, has_side_effects=True, vmem_limit_bytes=56 * 2**20
        ),
    )(features, sketch_matrix, tiles[0], tile_dst, tile_src, halo_index, send_order, arrival_place)


def solution(mesh):
    in_specs = (
        P(("dom", "rep"), None),
        P(),
        P("dom", None, None, None),
        P("dom", None),
        P("dom", None),
        P("dom", None),
        P("dom", None),
        P("dom", None),
    )
    return jax.shard_map(
        on_device, mesh=mesh, in_specs=in_specs, out_specs=P(None, "rep", "dom"), check_vma=False
    )
```
